32 devices in a mesh: fsdp: 32 (over z, y, x, core).
Axes of the slice: x: 2, y: 2, z: 4, core: 2. Of those that a mesh axis runs over, the one named last changes fastest.
Arguments:
- inputs: bfloat16 [32, 128, 960], P('fsdp'), may hold values from -6 to 6
- out_cotangent: bfloat16 [32, 128, 960], P('fsdp'), may hold values from -6 to 6
- attn_gain: float32 [960], replicated, may hold values from 0.5 to 1.5
- mlp_gain: float32 [960], replicated, may hold values from 0.5 to 1.5
- query_weight: bfloat16 [921600], P('fsdp'), may hold values from -0.1875 to 0.1875
- key_matrix: bfloat16 [307200], P('fsdp'), may hold values from -0.1875 to 0.1875
- value_matrix: bfloat16 [307200], P('fsdp'), may hold values from -0.1875 to 0.1875
- output_weight: bfloat16 [921600], P('fsdp'), may hold values from -0.5 to 0.5
- gate_weight: bfloat16 [2457600], P('fsdp'), may hold values from -0.1875 to 0.1875
- up_weight: bfloat16 [2457600], P('fsdp'), may hold values from -0.1875 to 0.1875
- down_weight: bfloat16 [2457600], P('fsdp'), may hold values from -0.125 to 0.125
Outputs:
- output: bfloat16 [32, 128, 960], P('fsdp')
- input_grad: float32 [32, 128, 960], P('fsdp')
- query_grad: float32 [921600], P('fsdp')
- key_grad: float32 [307200], P('fsdp')
- value_grad: float32 [307200], P('fsdp')
- output_grad: float32 [921600], P('fsdp')
- gate_grad: float32 [2457600], P('fsdp')
- up_grad: float32 [2457600], P('fsdp')
- down_grad: float32 [2457600], P('fsdp')
- attn_gain_grad: float32 [960], replicated
- mlp_gain_grad: float32 [960], replicated
The draws below stay inside these ranges and needn't reach their ends.
All inputs are finite; a program needn't handle non-finite values.
Results may differ from the reference program's by a relative error of at most 0.015.
Values may be sent and summed in bfloat16 or wider, within the bound.
A program may use at most 192 MiB of HBM per device.

```python
import jax
import jax.numpy as jnp
from jax import lax

MODEL_DIMENSION = 960
QUERY_HEADS = 15
KEY_VALUE_HEADS = 5
HEAD_DIMENSION = 64
FEEDFORWARD_SIZE = 2560
SEQ = 128
SEQS = 32


def shard_levels(own_key, dims, shards, low, largest):
    factor_of, own = 1.0, jax.random.fold_in(own_key, 6)
    for dim, shards_of in shards:
        heights = jnp.exp(jax.random.uniform(jax.random.fold_in(own, dim), (shards_of,), jnp.float32, low / len(shards), largest / len(shards)))
        factor_of = factor_of * jnp.repeat(heights, dims[dim] // shards_of).reshape([-1 if axis == dim else 1 for axis in range(len(dims))])
    return factor_of


def bell_draw(stream_key, shape, scale, bound, pieces=(), dtype=jnp.bfloat16):
    result = jax.random.normal(stream_key, shape, jnp.float32) * scale
    if len(pieces) > 0:
        result = shard_levels(stream_key, shape, pieces, -0.22, 0.18) * result
    return jnp.clip(result, min=-bound, max=bound).astype(dtype)


def setup_inputs(seed: int = 0) -> dict:
    key_list = jax.random.split(jax.random.key(seed), 12)
    return {
        "inputs": bell_draw(key_list[0], (SEQS, SEQ, MODEL_DIMENSION), 1.0, 6.0, ((0, 32),)),
        "out_cotangent": bell_draw(key_list[1], (SEQS, SEQ, MODEL_DIMENSION), 1.0, 6.0, ((0, 32),)),
        "attn_gain": jnp.clip(1.0 + 0.1 * jax.random.normal(key_list[2], (MODEL_DIMENSION,), jnp.float32), 0.5, 1.5),
        "mlp_gain": jnp.clip(1.0 + 0.1 * jax.random.normal(key_list[3], (MODEL_DIMENSION,), jnp.float32), 0.5, 1.5),
        "query_weight": bell_draw(key_list[4], (MODEL_DIMENSION * QUERY_HEADS * HEAD_DIMENSION,), MODEL_DIMENSION ** -0.5, 0.1875, ((0, 32),)),
        "key_matrix": bell_draw(key_list[5], (MODEL_DIMENSION * KEY_VALUE_HEADS * HEAD_DIMENSION,), MODEL_DIMENSION ** -0.5, 0.1875, ((0, 32),)),
        "value_matrix": bell_draw(key_list[6], (MODEL_DIMENSION * KEY_VALUE_HEADS * HEAD_DIMENSION,), MODEL_DIMENSION ** -0.5, 0.1875, ((0, 32),)),
        "output_weight": bell_draw(key_list[7], (QUERY_HEADS * HEAD_DIMENSION * MODEL_DIMENSION,), (QUERY_HEADS * HEAD_DIMENSION // 8) ** -0.5, 0.5, ((0, 32),)),
        "gate_weight": bell_draw(key_list[8], (MODEL_DIMENSION * FEEDFORWARD_SIZE,), MODEL_DIMENSION ** -0.5, 0.1875, ((0, 32),)),
        "up_weight": bell_draw(key_list[9], (MODEL_DIMENSION * FEEDFORWARD_SIZE,), MODEL_DIMENSION ** -0.5, 0.1875, ((0, 32),)),
        "down_weight": bell_draw(key_list[10], (FEEDFORWARD_SIZE * MODEL_DIMENSION,), FEEDFORWARD_SIZE ** -0.5, 0.125, ((0, 32),)),
    }


EPS = 1e-05
THETA = 100000.0
MASKED = -1e+30

def rope_tables(sequence_length, half_width):
    position = jnp.arange(sequence_length).astype(jnp.float32)
    freqs = THETA ** (-(jnp.arange(half_width).astype(jnp.float32) * 2.0) / (2.0 * half_width))
    angle = position[:, None] * freqs[None, :]
    return (jnp.cos(angle)[:, None, :], jnp.sin(angle)[:, None, :])

def apply_rotary(tensor, cosine_lookup, sine_lookup, rotation_sign):
    half_width = tensor.shape[-1] // 2
    first = tensor[..., :half_width]
    second = tensor[..., half_width:]
    return jnp.concatenate([first * cosine_lookup - rotation_sign * second * sine_lookup, rotation_sign * first * sine_lookup + second * cosine_lookup], axis=-1)

def rounded_result(tensor):
    return lax.optimization_barrier(tensor.astype(jnp.bfloat16)).astype(jnp.float32)

def norm_forward(value_rows, gain):
    scale = lax.rsqrt(lax.optimization_barrier(jnp.mean(value_rows * value_rows, axis=-1, keepdims=True)) + EPS)
    unit = value_rows * scale
    return (unit, scale, (unit * gain).astype(jnp.bfloat16))

def norm_backward(d_normed, unit, scale, gain):
    d_unit = d_normed * gain
    d_input = scale * (d_unit - unit * lax.optimization_barrier(jnp.mean(d_unit * unit, axis=-1, keepdims=True)))
    return (d_input, lax.optimization_barrier(jnp.sum(d_normed * unit, axis=0)))

def multiply_matrices(left, right):
    return jnp.dot(left, right, preferred_element_type=jnp.float32)

def one_sequence(inputs, cotangent, attn_gain, mlp_gain, w_query, key_projection_full, value_projection_full, w_output, w_gate, w_up, w_down):
    sequence_length = inputs.shape[0]
    group_count = QUERY_HEADS // KEY_VALUE_HEADS
    factor = HEAD_DIMENSION ** (-0.5)
    cosine_lookup, sine_lookup = rope_tables(sequence_length, HEAD_DIMENSION // 2)
    causal = jnp.arange(sequence_length)[:, None] >= jnp.arange(sequence_length)[None, :]
    inputs_f32 = inputs.astype(jnp.float32)
    unit_one, scale_one, first_normalized = norm_forward(inputs_f32, attn_gain)
    query_rows = rounded_result(apply_rotary(multiply_matrices(first_normalized, w_query).reshape(sequence_length, QUERY_HEADS, HEAD_DIMENSION), cosine_lookup, sine_lookup, 1.0))
    key_rows = rounded_result(apply_rotary(multiply_matrices(first_normalized, key_projection_full).reshape(sequence_length, KEY_VALUE_HEADS, HEAD_DIMENSION), cosine_lookup, sine_lookup, 1.0))
    value_rows = rounded_result(multiply_matrices(first_normalized, value_projection_full).reshape(sequence_length, KEY_VALUE_HEADS, HEAD_DIMENSION))
    keys_rep = jnp.repeat(key_rows, group_count, axis=1)
    values_rep = jnp.repeat(value_rows, group_count, axis=1)
    scores = jnp.where(causal[None], jnp.einsum('qhd,khd->hqk', query_rows, keys_rep) * factor, MASKED)
    row_top = lax.optimization_barrier(jnp.max(scores, axis=-1, keepdims=True))
    log_total = row_top + jnp.log(lax.optimization_barrier(jnp.sum(jnp.exp(scores - row_top), axis=-1, keepdims=True)))
    probs = rounded_result(jnp.exp(scores - log_total))
    attended = jnp.einsum('hqk,khd->qhd', probs, values_rep).astype(jnp.bfloat16).reshape(sequence_length, QUERY_HEADS * HEAD_DIMENSION)
    hidden = inputs_f32 + multiply_matrices(attended, w_output)
    unit_two, scale_two, normed_two = norm_forward(hidden, mlp_gain)
    gate = multiply_matrices(normed_two, w_gate)
    up_val = multiply_matrices(normed_two, w_up)
    sigmoid_gate = jax.nn.sigmoid(gate)
    activated = gate * sigmoid_gate
    mixed = (activated * up_val).astype(jnp.bfloat16)
    output = (hidden + multiply_matrices(mixed, w_down)).astype(jnp.bfloat16)
    d_down = multiply_matrices(mixed.T, cotangent)
    d_mixed = multiply_matrices(cotangent, w_down.T)
    d_gate = (d_mixed * up_val * (sigmoid_gate * (1.0 + gate * (1.0 - sigmoid_gate)))).astype(jnp.bfloat16)
    d_up = (d_mixed * activated).astype(jnp.bfloat16)
    d_gate_w = multiply_matrices(normed_two.T, d_gate)
    d_up_w = multiply_matrices(normed_two.T, d_up)
    d_normed_two = multiply_matrices(d_gate, w_gate.T) + multiply_matrices(d_up, w_up.T)
    d_hid_norm, d_mlp_gain = norm_backward(d_normed_two, unit_two, scale_two, mlp_gain)
    d_hidden = cotangent.astype(jnp.float32) + d_hid_norm
    d_branch = d_hidden.astype(jnp.bfloat16)
    d_output_w = multiply_matrices(attended.T, d_branch)
    attended_gradient = rounded_result(multiply_matrices(d_branch, w_output.T).reshape(sequence_length, QUERY_HEADS, HEAD_DIMENSION))
    d_probs = jnp.einsum('qhd,khd->hqk', attended_gradient, values_rep)
    repeated_value_gradient = jnp.einsum('hqk,qhd->khd', probs, attended_gradient)
    delta = lax.optimization_barrier(jnp.sum(probs * d_probs, axis=-1, keepdims=True))
    d_scores = rounded_result(probs * (d_probs - delta) * factor)
    d_queries = jnp.einsum('hqk,khd->qhd', d_scores, keys_rep)
    repeated_key_gradient = jnp.einsum('hqk,qhd->khd', d_scores, query_rows)
    key_rows_gradient = lax.optimization_barrier(jnp.sum(repeated_key_gradient.reshape(sequence_length, KEY_VALUE_HEADS, group_count, HEAD_DIMENSION), axis=2))
    value_rows_gradient = lax.optimization_barrier(jnp.sum(repeated_value_gradient.reshape(sequence_length, KEY_VALUE_HEADS, group_count, HEAD_DIMENSION), axis=2))
    d_query_in = apply_rotary(d_queries, cosine_lookup, sine_lookup, -1.0).reshape(sequence_length, QUERY_HEADS * HEAD_DIMENSION).astype(jnp.bfloat16)
    key_input_gradient = apply_rotary(key_rows_gradient, cosine_lookup, sine_lookup, -1.0).reshape(sequence_length, KEY_VALUE_HEADS * HEAD_DIMENSION).astype(jnp.bfloat16)
    value_input_gradient = value_rows_gradient.reshape(sequence_length, KEY_VALUE_HEADS * HEAD_DIMENSION).astype(jnp.bfloat16)
    d_query_w = multiply_matrices(first_normalized.T, d_query_in)
    d_key_w = multiply_matrices(first_normalized.T, key_input_gradient)
    d_value_w = multiply_matrices(first_normalized.T, value_input_gradient)
    d_normed_one = multiply_matrices(d_query_in, w_query.T) + multiply_matrices(key_input_gradient, key_projection_full.T) + multiply_matrices(value_input_gradient, value_projection_full.T)
    d_in_norm, d_attn_gain = norm_backward(d_normed_one, unit_one, scale_one, attn_gain)
    input_grad = d_hidden + d_in_norm
    grads = (d_query_w, d_key_w, d_value_w, d_output_w, d_gate_w, d_up_w, d_down, d_attn_gain, d_mlp_gain)
    return (output, input_grad, grads)

def reference(inputs, out_cotangent, attn_gain, mlp_gain, query_weight, key_matrix, value_matrix, output_weight, gate_weight, up_weight, down_weight):
    w_query = query_weight.reshape(MODEL_DIMENSION, QUERY_HEADS * HEAD_DIMENSION)
    key_projection_full = key_matrix.reshape(MODEL_DIMENSION, KEY_VALUE_HEADS * HEAD_DIMENSION)
    value_projection_full = value_matrix.reshape(MODEL_DIMENSION, KEY_VALUE_HEADS * HEAD_DIMENSION)
    w_output = output_weight.reshape(QUERY_HEADS * HEAD_DIMENSION, MODEL_DIMENSION)
    w_gate = gate_weight.reshape(MODEL_DIMENSION, FEEDFORWARD_SIZE)
    w_up = up_weight.reshape(MODEL_DIMENSION, FEEDFORWARD_SIZE)
    w_down = down_weight.reshape(FEEDFORWARD_SIZE, MODEL_DIMENSION)
    starting_value = (jnp.zeros((MODEL_DIMENSION, QUERY_HEADS * HEAD_DIMENSION), jnp.float32), jnp.zeros((MODEL_DIMENSION, KEY_VALUE_HEADS * HEAD_DIMENSION), jnp.float32), jnp.zeros((MODEL_DIMENSION, KEY_VALUE_HEADS * HEAD_DIMENSION), jnp.float32), jnp.zeros((QUERY_HEADS * HEAD_DIMENSION, MODEL_DIMENSION), jnp.float32), jnp.zeros((MODEL_DIMENSION, FEEDFORWARD_SIZE), jnp.float32), jnp.zeros((MODEL_DIMENSION, FEEDFORWARD_SIZE), jnp.float32), jnp.zeros((FEEDFORWARD_SIZE, MODEL_DIMENSION), jnp.float32), jnp.zeros((MODEL_DIMENSION,), jnp.float32), jnp.zeros((MODEL_DIMENSION,), jnp.float32))

    def accumulate(totals, pair):
        seq_inputs, seq_cotangent = pair
        output, input_grad, grads = one_sequence(seq_inputs, seq_cotangent, attn_gain, mlp_gain, w_query, key_projection_full, value_projection_full, w_output, w_gate, w_up, w_down)
        return (jax.tree.map(lambda first, second: first + second, totals, grads), (output, input_grad))
    totals, outs = lax.scan(accumulate, starting_value, (inputs, out_cotangent))
    return (outs[0], outs[1], totals[0].reshape(-1), totals[1].reshape(-1), totals[2].reshape(-1), totals[3].reshape(-1), totals[4].reshape(-1), totals[5].reshape(-1), totals[6].reshape(-1), totals[7], totals[8])
```

```python
import functools

import jax
import jax.numpy as jnp
from jax import lax
from jax.experimental import pallas as pl
from jax.experimental.pallas import tpu as pltpu
from jax.sharding import PartitionSpec as P

QUERY_HEADS = 15
KEY_VALUE_HEADS = 5
HEAD_DIMENSION = 64
FEEDFORWARD_SIZE = 2560


EPS = 1e-05
THETA = 100000.0
MASKED = -1e30


def rope_tables(sequence_length, half_width):
    position = jnp.arange(sequence_length).astype(jnp.float32)
    freqs = THETA ** (-(jnp.arange(half_width).astype(jnp.float32) * 2.0) / (2.0 * half_width))
    angle = position[:, None] * freqs[None, :]
    return (jnp.cos(angle)[:, None, :], jnp.sin(angle)[:, None, :])


def apply_rotary(tensor, cosine_lookup, sine_lookup, rotation_sign):
    half_width = tensor.shape[-1] // 2
    first = tensor[..., :half_width]
    second = tensor[..., half_width:]
    return jnp.concatenate(
        [
            first * cosine_lookup - rotation_sign * second * sine_lookup,
            rotation_sign * first * sine_lookup + second * cosine_lookup,
        ],
        axis=-1,
    )


def norm_forward(value_rows, gain):
    scale = lax.rsqrt(jnp.mean(value_rows * value_rows, axis=-1, keepdims=True) + EPS)
    unit = value_rows * scale
    return (unit, scale, (unit * gain).astype(jnp.bfloat16))


def norm_backward(d_normed, unit, scale, gain):
    d_unit = d_normed * gain
    d_input = scale * (d_unit - unit * jnp.mean(d_unit * unit, axis=-1, keepdims=True))
    return (d_input, jnp.sum(d_normed * unit, axis=0))


def matrix_product(left, right):
    return jnp.dot(left, right, preferred_element_type=jnp.float32)


def back_product(left, right):
    return jnp.einsum("tf,df->td", left, right, preferred_element_type=jnp.float32)


def masked_scores(query_rows, key_rows, causal, factor):
    raw = (
        jnp.einsum("bqngd,bknd->bngqk", query_rows, key_rows, preferred_element_type=jnp.float32)
        * factor
    )
    return jnp.where(causal[None, None, None], raw, MASKED)


def flat_slice(left, right, count, stretch):
    product = jnp.einsum("tr,tf->rf", left, right, preferred_element_type=jnp.float32).reshape(-1)
    return product.reshape(count, stretch)


def gradient_term(pairs, devices, count):
    return jnp.concatenate(
        [
            flat_slice(left, right, count, left.shape[1] * right.shape[1] // devices)
            for left, right in pairs
        ],
        axis=1,
    )


def split_shards(joined, pairs, devices):
    pieces = []
    offset = 0
    for left, right in pairs:
        stretch = left.shape[1] * right.shape[1] // devices
        pieces.append(joined[0, offset : offset + stretch])
        offset = offset + stretch
    return pieces


def body(
    inputs,
    out_cotangent,
    attn_gain,
    mlp_gain,
    query_weight,
    key_matrix,
    value_matrix,
    output_weight,
    gate_weight,
    up_weight,
    down_weight,
):
    batch_count, sequence_length, model_width = inputs.shape
    row_count = batch_count * sequence_length
    devices = lax.axis_size("fsdp")
    group_count = QUERY_HEADS // KEY_VALUE_HEADS
    q_width = QUERY_HEADS * HEAD_DIMENSION
    key_value_width = KEY_VALUE_HEADS * HEAD_DIMENSION
    factor = HEAD_DIMENSION ** (-0.5)
    cosine_lookup, sine_lookup = rope_tables(sequence_length, HEAD_DIMENSION // 2)
    causal = jnp.arange(sequence_length)[:, None] >= jnp.arange(sequence_length)[None, :]
    full_query, full_key, full_value, full_output = (
        lax.all_gather(query_weight, "fsdp", axis=0, tiled=True),
        lax.all_gather(key_matrix, "fsdp", axis=0, tiled=True),
        lax.all_gather(value_matrix, "fsdp", axis=0, tiled=True),
        lax.all_gather(output_weight, "fsdp", axis=0, tiled=True),
    )
    w_query = full_query.reshape(model_width, q_width)
    key_projection_full = full_key.reshape(model_width, key_value_width)
    value_projection_full = full_value.reshape(model_width, key_value_width)
    w_output = full_output.reshape(q_width, model_width)
    inputs_f32 = inputs.reshape(row_count, model_width).astype(jnp.float32)
    unit_one, scale_one, first_normalized = norm_forward(inputs_f32, attn_gain)
    query_rows = apply_rotary(
        matrix_product(first_normalized, w_query).reshape(
            batch_count, sequence_length, QUERY_HEADS, HEAD_DIMENSION
        ),
        cosine_lookup,
        sine_lookup,
        1.0,
    )
    query_rows = query_rows.astype(jnp.bfloat16).reshape(
        batch_count, sequence_length, KEY_VALUE_HEADS, group_count, HEAD_DIMENSION
    )
    key_rows = apply_rotary(
        matrix_product(first_normalized, key_projection_full).reshape(
            batch_count, sequence_length, KEY_VALUE_HEADS, HEAD_DIMENSION
        ),
        cosine_lookup,
        sine_lookup,
        1.0,
    )
    key_rows = key_rows.astype(jnp.bfloat16)
    value_rows = (
        matrix_product(first_normalized, value_projection_full)
        .astype(jnp.bfloat16)
        .reshape(batch_count, sequence_length, KEY_VALUE_HEADS, HEAD_DIMENSION)
    )
    scores = masked_scores(query_rows, key_rows, causal, factor)
    row_top = jnp.max(scores, axis=-1, keepdims=True)
    log_total = row_top + jnp.log(jnp.sum(jnp.exp(scores - row_top), axis=-1, keepdims=True))
    probs = jnp.exp(scores - log_total).astype(jnp.bfloat16)
    attended = jnp.einsum(
        "bngqk,bknd->bqngd", probs, value_rows, preferred_element_type=jnp.float32
    )
    attended = attended.astype(jnp.bfloat16).reshape(row_count, q_width)
    hidden = inputs_f32 + matrix_product(attended, w_output)
    full_gate, full_up, full_down = (
        lax.all_gather(gate_weight, "fsdp", axis=0, tiled=True),
        lax.all_gather(up_weight, "fsdp", axis=0, tiled=True),
        lax.all_gather(down_weight, "fsdp", axis=0, tiled=True),
    )
    w_gate = full_gate.reshape(model_width, FEEDFORWARD_SIZE)
    w_up = full_up.reshape(model_width, FEEDFORWARD_SIZE)
    w_down = full_down.reshape(FEEDFORWARD_SIZE, model_width)
    unit_two, scale_two, normed_two = norm_forward(hidden, mlp_gain)
    gate = matrix_product(normed_two, w_gate)
    up_val = matrix_product(normed_two, w_up)
    sigmoid_gate = jax.nn.sigmoid(gate)
    activated = gate * sigmoid_gate
    mixed = (activated * up_val).astype(jnp.bfloat16)
    output = (
        (hidden + matrix_product(mixed, w_down))
        .astype(jnp.bfloat16)
        .reshape(batch_count, sequence_length, model_width)
    )
    again_gate, again_up, again_down = (
        lax.all_gather(gate_weight, "fsdp", axis=0, tiled=True),
        lax.all_gather(up_weight, "fsdp", axis=0, tiled=True),
        lax.all_gather(down_weight, "fsdp", axis=0, tiled=True),
    )
    w_gate = again_gate.reshape(model_width, FEEDFORWARD_SIZE)
    w_up = again_up.reshape(model_width, FEEDFORWARD_SIZE)
    w_down = again_down.reshape(FEEDFORWARD_SIZE, model_width)
    cotangent = out_cotangent.reshape(row_count, model_width)
    d_mixed = back_product(cotangent, w_down)
    d_gate = (d_mixed * up_val * (sigmoid_gate * (1.0 + gate * (1.0 - sigmoid_gate)))).astype(
        jnp.bfloat16
    )
    d_up = (d_mixed * activated).astype(jnp.bfloat16)
    mlp_pairs = [(normed_two, d_gate), (normed_two, d_up), (mixed, cotangent)]
    mlp_joined = lax.psum_scatter(
        gradient_term(mlp_pairs, devices, lax.axis_size("fsdp") * 1),
        "fsdp",
        scatter_dimension=0,
        tiled=True,
    )
    mlp_shards = split_shards(mlp_joined, mlp_pairs, devices)
    d_normed_two = back_product(d_gate, w_gate) + back_product(d_up, w_up)
    d_hid_norm, d_mlp_gain = norm_backward(d_normed_two, unit_two, scale_two, mlp_gain)
    d_hidden = cotangent.astype(jnp.float32) + d_hid_norm
    d_branch = d_hidden.astype(jnp.bfloat16)
    again_query, again_key, again_value, again_output = (
        lax.all_gather(query_weight, "fsdp", axis=0, tiled=True),
        lax.all_gather(key_matrix, "fsdp", axis=0, tiled=True),
        lax.all_gather(value_matrix, "fsdp", axis=0, tiled=True),
        lax.all_gather(output_weight, "fsdp", axis=0, tiled=True),
    )
    w_query = again_query.reshape(model_width, q_width)
    key_projection_full = again_key.reshape(model_width, key_value_width)
    value_projection_full = again_value.reshape(model_width, key_value_width)
    w_output = again_output.reshape(q_width, model_width)
    attended_gradient = back_product(d_branch, w_output).astype(jnp.bfloat16)
    attended_gradient = attended_gradient.reshape(
        batch_count, sequence_length, KEY_VALUE_HEADS, group_count, HEAD_DIMENSION
    )
    scores_again = masked_scores(query_rows, key_rows, causal, factor)
    probs_again = jnp.exp(scores_again - log_total).astype(jnp.bfloat16)
    d_probs = jnp.einsum(
        "bqngd,bknd->bngqk", attended_gradient, value_rows, preferred_element_type=jnp.float32
    )
    value_rows_gradient = jnp.einsum(
        "bngqk,bqngd->bknd", probs_again, attended_gradient, preferred_element_type=jnp.float32
    )
    probs_f32 = probs_again.astype(jnp.float32)
    delta = jnp.sum(probs_f32 * d_probs, axis=-1, keepdims=True)
    d_scores = (probs_f32 * (d_probs - delta) * factor).astype(jnp.bfloat16)
    d_queries = jnp.einsum(
        "bngqk,bknd->bqngd", d_scores, key_rows, preferred_element_type=jnp.float32
    )
    key_rows_gradient = jnp.einsum(
        "bngqk,bqngd->bknd", d_scores, query_rows, preferred_element_type=jnp.float32
    )
    d_queries = d_queries.reshape(batch_count, sequence_length, QUERY_HEADS, HEAD_DIMENSION)
    d_query_in = (
        apply_rotary(d_queries, cosine_lookup, sine_lookup, -1.0)
        .reshape(row_count, q_width)
        .astype(jnp.bfloat16)
    )
    key_input_gradient = (
        apply_rotary(key_rows_gradient, cosine_lookup, sine_lookup, -1.0)
        .reshape(row_count, key_value_width)
        .astype(jnp.bfloat16)
    )
    value_input_gradient = value_rows_gradient.reshape(row_count, key_value_width).astype(
        jnp.bfloat16
    )
    d_normed_one = (
        back_product(d_query_in, w_query)
        + back_product(key_input_gradient, key_projection_full)
        + back_product(value_input_gradient, value_projection_full)
    )
    d_in_norm, d_attn_gain = norm_backward(d_normed_one, unit_one, scale_one, attn_gain)
    input_grad = (d_hidden + d_in_norm).reshape(batch_count, sequence_length, model_width)
    attn_pairs = [
        (first_normalized, d_query_in),
        (first_normalized, key_input_gradient),
        (first_normalized, value_input_gradient),
        (attended, d_branch),
    ]
    attn_joined = lax.psum_scatter(
        gradient_term(attn_pairs, devices, lax.axis_size("fsdp") * 1),
        "fsdp",
        scatter_dimension=0,
        tiled=True,
    )
    shards = split_shards(attn_joined, attn_pairs, devices) + mlp_shards
    gain_sums = lax.psum((d_attn_gain, d_mlp_gain), "fsdp")
    return (
        output,
        input_grad,
        shards[0],
        shards[1],
        shards[2],
        shards[3],
        shards[4],
        shards[5],
        shards[6],
        gain_sums[0],
        gain_sums[1],
    )


PLANES = 4
TILE = 16


def unit_place(me):
    return me // 8, (me // 4) % 2, (me // 2) % 2, me % 2


def unit_index(z, y, x, c):
    return ((z * 2 + y) * 2 + x) * 2 + c


def partners(me):
    z, y, x, c = unit_place(me)
    peers = [unit_index((z + k) % PLANES, y, x, c) for k in range(1, PLANES)]
    peers.append(unit_index(z, y, 1 - x, c))
    peers.append(unit_index(z, 1 - y, x, c))
    peers.append(unit_index(z, y, x, 1 - c))
    return peers


def meet(peers):
    barrier = pltpu.get_barrier_semaphore()
    for peer in peers:
        pl.semaphore_signal(
            barrier, inc=1, device_id=(peer,), device_id_type=pl.DeviceIdType.MESH
        )
    pl.semaphore_wait(barrier, len(peers))


def remote(source, target, send, receive, device):
    return pltpu.make_async_remote_copy(
        src_ref=source,
        dst_ref=target,
        send_sem=send,
        recv_sem=receive,
        device_id=(device,),
        device_id_type=pl.DeviceIdType.MESH,
    )


def gather_kernel(count, *refs):
    shards, wholes = refs[:count], refs[count : 2 * count]
    send, receive, local = refs[2 * count :]
    me = lax.axis_index("fsdp")
    z, y, x, c = unit_place(me)
    meet(partners(me))

    def copies(a, phase):
        whole = wholes[a]
        x_first = a % 2 == 0
        if phase == 0:
            return [
                remote(
                    shards[a],
                    whole.at[z, y, x, c],
                    send.at[a, k - 1],
                    receive.at[a, k - 1],
                    unit_index((z + k) % PLANES, y, x, c),
                )
                for k in range(1, PLANES)
            ]
        over_x = unit_index(z, y, 1 - x, c)
        over_y = unit_index(z, 1 - y, x, c)
        if phase == 1:
            part, device = whole.at[:, y, x, c], (over_x if x_first else over_y)
        elif phase == 2:
            part = whole.at[:, y, :, c] if x_first else whole.at[:, :, x, c]
            device = over_y if x_first else over_x
        else:
            part, device = whole.at[:, :, :, c], unit_index(z, y, x, 1 - c)
        return [remote(part, part, send.at[a, phase + 2], receive.at[a, phase + 2], device)]

    locals_ = [
        pltpu.make_async_copy(shards[a], wholes[a].at[z, y, x, c], local.at[a])
        for a in range(count)
    ]
    for a in range(count):
        for copy in copies(a, 0):
            copy.start()
        locals_[a].start()
    for step in range(count + 3):
        for phase in (3, 2, 1):
            a = step - (phase - 1)
            if 0 <= a < count:
                if phase == 1:
                    locals_[a].wait()
                for copy in copies(a, phase - 1):
                    copy.wait_recv()
                for copy in copies(a, phase):
                    copy.start()
    for a in range(count):
        for copy in copies(a, 3):
            copy.wait_recv()
        for phase in range(4):
            for copy in copies(a, phase):
                copy.wait_send()


def gather_blocks(shards, identity):
    count = len(shards)
    return pl.pallas_call(
        functools.partial(gather_kernel, count),
        out_shape=[jax.ShapeDtypeStruct((PLANES, 2, 2, 2) + s.shape, s.dtype) for s in shards],
        in_specs=[pl.BlockSpec(memory_space=pl.ANY)] * count,
        out_specs=[pl.BlockSpec(memory_space=pl.ANY)] * count,
        scratch_shapes=[
            pltpu.SemaphoreType.DMA((count, 6)),
            pltpu.SemaphoreType.DMA((count, 6)),
            pltpu.SemaphoreType.DMA((count,)),
        ],
        compiler_params=pltpu.CompilerParams(collective_id=identity, has_side_effects=True),
    )(*shards)


def scatter_kernel(count, *refs):
    grads, gain = refs[:count], refs[count]
    outs, gain_out = refs[count + 1 : 2 * count + 1], refs[2 * count + 1]
    rest = refs[2 * count + 2 :]
    held, sibling, second, third, last = (rest[i * count : (i + 1) * count] for i in range(5))
    gain_a, gain_b, gain_c, gain_z, send, receive, local = rest[5 * count :]
    me = lax.axis_index("fsdp")
    z, y, x, c = unit_place(me)
    meet(partners(me))
    over_core = unit_index(z, y, x, 1 - c)
    over_x = unit_index(z, y, 1 - x, c)
    over_y = unit_index(z, 1 - y, x, c)

    def copies(a, phase):
        x_first = a % 2 == 0
        if phase == 0:
            jobs = [(grads[a].at[:, :, :, 1 - c], sibling[a], over_core)]
        elif phase == 1:
            if x_first:
                jobs = [(held[a].at[:, :, 1 - x], second[a], over_x)]
            else:
                jobs = [(held[a].at[:, 1 - y], second[a], over_y)]
        elif phase == 2:
            if x_first:
                jobs = [(held[a].at[:, 1 - y, x], third[a], over_y)]
            else:
                jobs = [(held[a].at[:, y, 1 - x], third[a], over_x)]
        else:
            jobs = []
            for k in range(1, PLANES):
                to = (z + k) % PLANES
                jobs.append((held[a].at[to, y, x], last[a].at[k - 1], unit_index(to, y, x, c)))
        return [
            remote(s, d, send.at[a, phase + i], receive.at[a, phase + i], device)
            for i, (s, d, device) in enumerate(jobs)
        ]

    def add(target, term):
        target[...] = (target[...].astype(jnp.float32) + term[...].astype(jnp.float32)).astype(
            target.dtype
        )

    def fold(a, phase):
        x_first = a % 2 == 0
        if phase == 0:

            @pl.loop(0, PLANES * 4)
            def _(i):
                zz, yy, xx = i // 4, (i // 2) % 2, i % 2
                add(held[a].at[zz, yy, xx], sibling[a].at[zz, yy, xx])

        elif phase == 1:

            @pl.loop(0, PLANES * 2)
            def _(i):
                zz, other = i // 2, i % 2
                if x_first:
                    add(held[a].at[zz, other, x], second[a].at[zz, other])
                else:
                    add(held[a].at[zz, y, other], second[a].at[zz, other])

        elif phase == 2:

            @pl.loop(0, PLANES)
            def _(zz):
                add(held[a].at[zz, y, x], third[a].at[zz])

        else:
            total = held[a][z, y, x].astype(jnp.float32)
            for k in range(PLANES - 1):
                total = total + last[a][k].astype(jnp.float32)
            outs[a][...] = total

    def gain_copies(phase):
        if phase < 3:
            source, target, device = (
                (gain, gain_a.at[1], over_core),
                (gain_a.at[0], gain_b.at[1], over_x),
                (gain_b.at[0], gain_c, over_y),
            )[phase]
            jobs = [(source, target, device)]
        else:
            jobs = [
                (gain_z.at[z], gain_z.at[z], unit_index((z + k) % PLANES, y, x, c))
                for k in range(1, PLANES)
            ]
        return [
            remote(s, d, send.at[count, phase + i], receive.at[count, phase + i], device)
            for i, (s, d, device) in enumerate(jobs)
        ]

    def gain_fold(phase):
        if phase == 0:
            gain_a[0] = gain[...] + gain_a[1]
        elif phase == 1:
            gain_b[0] = gain_a[0] + gain_b[1]
        elif phase == 2:
            gain_z[z] = gain_b[0] + gain_c[...]
        else:
            gain_out[...] = (gain_z[0] + gain_z[1]) + (gain_z[2] + gain_z[3])

    locals_ = [
        pltpu.make_async_copy(grads[a].at[:, :, :, c], held[a], local.at[a]) for a in range(count)
    ]
    for copy in gain_copies(0):
        copy.start()
    for a in range(count):
        for copy in copies(a, 0):
            copy.start()
        locals_[a].start()
    for step in range(count + 3):
        for phase in (3, 2, 1, 0):
            a = step - phase
            if 0 <= a < count:
                if phase == 0:
                    locals_[a].wait()
                for copy in copies(a, phase):
                    copy.wait_recv()
                fold(a, phase)
                if phase < 3:
                    for copy in copies(a, phase + 1):
                        copy.start()
        if step < 4:
            for copy in gain_copies(step):
                copy.wait_recv()
            gain_fold(step)
            if step < 3:
                for copy in gain_copies(step + 1):
                    copy.start()
    for phase in range(4):
        for a in range(count):
            for copy in copies(a, phase):
                copy.wait_send()
        for copy in gain_copies(phase):
            copy.wait_send()


def scatter_blocks(grads, gain, identity):
    count = len(grads)
    blocks = [g.shape[4:] for g in grads]
    kind = grads[0].dtype
    vmem = pl.BlockSpec(memory_space=pltpu.VMEM)

    def room(lead):
        return [pltpu.VMEM(lead + b, kind) for b in blocks]

    return pl.pallas_call(
        functools.partial(scatter_kernel, count),
        out_shape=[jax.ShapeDtypeStruct(b, jnp.float32) for b in blocks]
        + [jax.ShapeDtypeStruct(gain.shape, gain.dtype)],
        in_specs=[pl.BlockSpec(memory_space=pl.ANY)] * count + [vmem],
        out_specs=[vmem] * (count + 1),
        scratch_shapes=room((PLANES, 2, 2))
        + room((PLANES, 2, 2))
        + room((PLANES, 2))
        + room((PLANES,))
        + room((PLANES - 1,))
        + [
            pltpu.VMEM((2,) + gain.shape, gain.dtype),
            pltpu.VMEM((2,) + gain.shape, gain.dtype),
            pltpu.VMEM(gain.shape, gain.dtype),
            pltpu.VMEM((PLANES,) + gain.shape, gain.dtype),
            pltpu.SemaphoreType.DMA((count + 1, 6)),
            pltpu.SemaphoreType.DMA((count + 1, 6)),
            pltpu.SemaphoreType.DMA((count,)),
        ],
        compiler_params=pltpu.CompilerParams(
            collective_id=identity, has_side_effects=True, vmem_limit_bytes=48 * 1024 * 1024
        ),
    )(*grads, gain)


def spread_matrix(width, rows, padded_rows, devices):
    feature = jnp.arange(width)
    place = (feature // rows) * padded_rows + feature % rows
    return (place[:, None] == jnp.arange(devices * padded_rows)[None, :]).astype(jnp.bfloat16)


def widen(rows, spread):
    return matrix_product(rows.astype(jnp.bfloat16), spread).astype(jnp.bfloat16)


def narrow_exact(rows, spread):
    high = lax.reduce_precision(rows, 8, 7)
    middle = lax.reduce_precision(rows - high, 8, 7)
    low = rows - high - middle
    stacked = jnp.concatenate([high, middle, low], axis=0).astype(jnp.bfloat16)
    stacked = back_product(stacked, spread)
    count = rows.shape[0]
    return stacked[:count] + (stacked[count : 2 * count] + stacked[2 * count :])


def fast_body(
    inputs,
    out_cotangent,
    attn_gain,
    mlp_gain,
    query_weight,
    key_matrix,
    value_matrix,
    output_weight,
    gate_weight,
    up_weight,
    down_weight,
):
    _, sequence_length, model_width = inputs.shape
    tokens = sequence_length
    devices = lax.axis_size("fsdp")
    groups = QUERY_HEADS // KEY_VALUE_HEADS
    q_width = QUERY_HEADS * HEAD_DIMENSION
    kv_width = KEY_VALUE_HEADS * HEAD_DIMENSION
    factor = HEAD_DIMENSION ** (-0.5)
    rows = model_width // devices
    padded = -(-rows // TILE) * TILE
    down_rows = FEEDFORWARD_SIZE // devices
    cosine, sine = rope_tables(sequence_length, HEAD_DIMENSION // 2)
    causal = jnp.arange(sequence_length)[:, None] >= jnp.arange(sequence_length)[None, :]
    spread = spread_matrix(model_width, rows, padded, devices)

    def lay(weight):
        return weight.reshape(rows, -1)

    def fill(matrix):
        return jnp.pad(matrix, ((0, padded - rows), (0, 0)))

    attn_shard = fill(
        jnp.concatenate(
            [lay(query_weight), lay(key_matrix), lay(value_matrix), lay(output_weight)], axis=1
        )
    )
    gathered = gather_blocks(
        [
            attn_shard,
            fill(lay(gate_weight)),
            fill(lay(up_weight)),
            down_weight.reshape(down_rows, model_width),
        ],
        0,
    )
    attn_all, w_gate, w_up, w_down = (g.reshape(-1, g.shape[-1]) for g in gathered)
    w_qkv = attn_all[:, : q_width + 2 * kv_width]
    w_output = attn_all[:, q_width + 2 * kv_width :]

    x = inputs.reshape(tokens, model_width).astype(jnp.float32)
    cotangent = out_cotangent.reshape(tokens, model_width)
    unit_one, scale_one, normed_one = norm_forward(x, attn_gain)
    normed_one = widen(normed_one, spread)
    qkv = matrix_product(normed_one, w_qkv)
    queries = apply_rotary(
        qkv[:, :q_width].reshape(tokens, QUERY_HEADS, HEAD_DIMENSION), cosine, sine, 1.0
    )
    queries = queries.astype(jnp.bfloat16).reshape(1, tokens, KEY_VALUE_HEADS, groups, HEAD_DIMENSION)
    keys = apply_rotary(
        qkv[:, q_width : q_width + kv_width].reshape(tokens, KEY_VALUE_HEADS, HEAD_DIMENSION),
        cosine,
        sine,
        1.0,
    )
    keys = keys.astype(jnp.bfloat16)[None]
    values = (
        qkv[:, q_width + kv_width :]
        .astype(jnp.bfloat16)
        .reshape(1, tokens, KEY_VALUE_HEADS, HEAD_DIMENSION)
    )
    scores = masked_scores(queries, keys, causal, factor)
    row_top = jnp.max(scores, axis=-1, keepdims=True)
    log_total = row_top + jnp.log(jnp.sum(jnp.exp(scores - row_top), axis=-1, keepdims=True))
    probs = jnp.exp(scores - log_total).astype(jnp.bfloat16)
    attended = jnp.einsum("bngqk,bknd->bqngd", probs, values, preferred_element_type=jnp.float32)
    attended = widen(attended.astype(jnp.bfloat16).reshape(tokens, q_width), spread)
    hidden = x + matrix_product(attended, w_output)
    unit_two, scale_two, normed_two = norm_forward(hidden, mlp_gain)
    normed_two = widen(normed_two, spread)
    gate = matrix_product(normed_two, w_gate)
    up_val = matrix_product(normed_two, w_up)
    sigmoid_gate = jax.nn.sigmoid(gate)
    activated = gate * sigmoid_gate
    mixed = (activated * up_val).astype(jnp.bfloat16)
    output = (hidden + matrix_product(mixed, w_down)).astype(jnp.bfloat16)
    d_mixed = back_product(cotangent, w_down)
    d_gate = (d_mixed * up_val * (sigmoid_gate * (1.0 + gate * (1.0 - sigmoid_gate)))).astype(
        jnp.bfloat16
    )
    d_up = (d_mixed * activated).astype(jnp.bfloat16)

    def weight_term(left, right):
        return jnp.einsum("tr,tf->rf", left, right, preferred_element_type=jnp.float32).astype(
            jnp.bfloat16
        )

    gate_term = weight_term(normed_two, d_gate)
    up_term = weight_term(normed_two, d_up)
    down_term = weight_term(mixed, cotangent)
    d_normed_two = narrow_exact(back_product(d_gate, w_gate) + back_product(d_up, w_up), spread)
    d_hid_norm, d_mlp_gain = norm_backward(d_normed_two, unit_two, scale_two, mlp_gain)
    d_hidden = cotangent.astype(jnp.float32) + d_hid_norm
    d_branch = d_hidden.astype(jnp.bfloat16)
    d_attended = back_product(d_branch, w_output).astype(jnp.bfloat16)
    d_attended = back_product(d_attended, spread).astype(jnp.bfloat16)
    d_attended = d_attended.reshape(1, tokens, KEY_VALUE_HEADS, groups, HEAD_DIMENSION)
    d_probs = jnp.einsum("bqngd,bknd->bngqk", d_attended, values, preferred_element_type=jnp.float32)
    d_values = jnp.einsum("bngqk,bqngd->bknd", probs, d_attended, preferred_element_type=jnp.float32)
    probs_f32 = probs.astype(jnp.float32)
    delta = jnp.sum(probs_f32 * d_probs, axis=-1, keepdims=True)
    d_scores = (probs_f32 * (d_probs - delta) * factor).astype(jnp.bfloat16)
    d_queries = jnp.einsum("bngqk,bknd->bqngd", d_scores, keys, preferred_element_type=jnp.float32)
    d_keys = jnp.einsum("bngqk,bqngd->bknd", d_scores, queries, preferred_element_type=jnp.float32)
    d_query_in = apply_rotary(
        d_queries.reshape(tokens, QUERY_HEADS, HEAD_DIMENSION), cosine, sine, -1.0
    ).reshape(tokens, q_width)
    d_key_in = apply_rotary(
        d_keys.reshape(tokens, KEY_VALUE_HEADS, HEAD_DIMENSION), cosine, sine, -1.0
    ).reshape(tokens, kv_width)
    d_qkv = jnp.concatenate([d_query_in, d_key_in, d_values.reshape(tokens, kv_width)], axis=1)
    d_qkv = d_qkv.astype(jnp.bfloat16)
    d_normed_one = narrow_exact(back_product(d_qkv, w_qkv), spread)
    d_in_norm, d_attn_gain = norm_backward(d_normed_one, unit_one, scale_one, attn_gain)
    input_grad = d_hidden + d_in_norm
    attn_term = jnp.concatenate(
        [weight_term(normed_one, d_qkv), weight_term(attended, d_branch)], axis=1
    )
    gains = jnp.concatenate([d_attn_gain, d_mlp_gain])
    lanes = 128
    gain_rows = -(-gains.shape[0] // (8 * lanes)) * 8
    gains = jnp.pad(gains, (0, gain_rows * lanes - gains.shape[0])).reshape(gain_rows, lanes)

    def split(term):
        return term.reshape(PLANES, 2, 2, 2, term.shape[0] // devices, term.shape[1])

    attn_part, gate_part, up_part, down_part, gain_sum = scatter_blocks(
        [split(attn_term), split(gate_term), split(up_term), split(down_term)], gains, 1
    )
    attn_part = attn_part[:rows]
    gain_sum = gain_sum.reshape(-1)
    first, second = q_width, q_width + kv_width
    third = second + kv_width
    return (
        output.reshape(inputs.shape),
        input_grad.reshape(inputs.shape),
        attn_part[:, :first].reshape(-1),
        attn_part[:, first:second].reshape(-1),
        attn_part[:, second:third].reshape(-1),
        attn_part[:, third:].reshape(-1),
        gate_part[:rows].reshape(-1),
        up_part[:rows].reshape(-1),
        down_part.reshape(-1),
        gain_sum[:model_width],
        gain_sum[model_width : 2 * model_width],
    )


def solution(mesh):
    in_specs = (
        P("fsdp", None, None),
        P("fsdp", None, None),
        P(),
        P(),
        P("fsdp"),
        P("fsdp"),
        P("fsdp"),
        P("fsdp"),
        P("fsdp"),
        P("fsdp"),
        P("fsdp"),
    )
    out_specs = (
        P("fsdp", None, None),
        P("fsdp", None, None),
        P("fsdp"),
        P("fsdp"),
        P("fsdp"),
        P("fsdp"),
        P("fsdp"),
        P("fsdp"),
        P("fsdp"),
        P(),
        P(),
    )
    chosen = fast_body if mesh.shape["fsdp"] == 8 * PLANES else body
    return jax.shard_map(
        chosen, mesh=mesh, in_specs=in_specs, out_specs=out_specs, check_vma=False)
```

```python
import functools

import jax
import jax.numpy as jnp
from jax import lax
from jax.experimental import pallas as pl
from jax.experimental.pallas import tpu as pltpu
from jax.sharding import PartitionSpec as P

QUERY_HEADS = 15
KEY_VALUE_HEADS = 5
HEAD_DIMENSION = 64
FEEDFORWARD_SIZE = 2560


EPS = 1e-05
THETA = 100000.0
MASKED = -1e30


def rope_tables(sequence_length, half_width):
    position = jnp.arange(sequence_length).astype(jnp.float32)
    freqs = THETA ** (-(jnp.arange(half_width).astype(jnp.float32) * 2.0) / (2.0 * half_width))
    angle = position[:, None] * freqs[None, :]
    return (jnp.cos(angle)[:, None, :], jnp.sin(angle)[:, None, :])


def apply_rotary(tensor, cosine_lookup, sine_lookup, rotation_sign):
    half_width = tensor.shape[-1] // 2
    first = tensor[..., :half_width]
    second = tensor[..., half_width:]
    return jnp.concatenate(
        [
            first * cosine_lookup - rotation_sign * second * sine_lookup,
            rotation_sign * first * sine_lookup + second * cosine_lookup,
        ],
        axis=-1,
    )


def norm_forward(value_rows, gain):
    scale = lax.rsqrt(jnp.mean(value_rows * value_rows, axis=-1, keepdims=True) + EPS)
    unit = value_rows * scale
    return (unit, scale, (unit * gain).astype(jnp.bfloat16))


def norm_backward(d_normed, unit, scale, gain):
    d_unit = d_normed * gain
    d_input = scale * (d_unit - unit * jnp.mean(d_unit * unit, axis=-1, keepdims=True))
    return (d_input, jnp.sum(d_normed * unit, axis=0))


def matrix_product(left, right):
    return jnp.dot(left, right, preferred_element_type=jnp.float32)


def back_product(left, right):
    return jnp.einsum("tf,df->td", left, right, preferred_element_type=jnp.float32)


def masked_scores(query_rows, key_rows, causal, factor):
    raw = (
        jnp.einsum("bqngd,bknd->bngqk", query_rows, key_rows, preferred_element_type=jnp.float32)
        * factor
    )
    return jnp.where(causal[None, None, None], raw, MASKED)


def flat_slice(left, right, count, stretch):
    product = jnp.einsum("tr,tf->rf", left, right, preferred_element_type=jnp.float32).reshape(-1)
    return product.reshape(count, stretch)


def gradient_term(pairs, devices, count):
    return jnp.concatenate(
        [
            flat_slice(left, right, count, left.shape[1] * right.shape[1] // devices)
            for left, right in pairs
        ],
        axis=1,
    )


def split_shards(joined, pairs, devices):
    pieces = []
    offset = 0
    for left, right in pairs:
        stretch = left.shape[1] * right.shape[1] // devices
        pieces.append(joined[0, offset : offset + stretch])
        offset = offset + stretch
    return pieces


def body(
    inputs,
    out_cotangent,
    attn_gain,
    mlp_gain,
    query_weight,
    key_matrix,
    value_matrix,
    output_weight,
    gate_weight,
    up_weight,
    down_weight,
):
    batch_count, sequence_length, model_width = inputs.shape
    row_count = batch_count * sequence_length
    devices = lax.axis_size("fsdp")
    group_count = QUERY_HEADS // KEY_VALUE_HEADS
    q_width = QUERY_HEADS * HEAD_DIMENSION
    key_value_width = KEY_VALUE_HEADS * HEAD_DIMENSION
    factor = HEAD_DIMENSION ** (-0.5)
    cosine_lookup, sine_lookup = rope_tables(sequence_length, HEAD_DIMENSION // 2)
    causal = jnp.arange(sequence_length)[:, None] >= jnp.arange(sequence_length)[None, :]
    full_query, full_key, full_value, full_output = (
        lax.all_gather(query_weight, "fsdp", axis=0, tiled=True),
        lax.all_gather(key_matrix, "fsdp", axis=0, tiled=True),
        lax.all_gather(value_matrix, "fsdp", axis=0, tiled=True),
        lax.all_gather(output_weight, "fsdp", axis=0, tiled=True),
    )
    w_query = full_query.reshape(model_width, q_width)
    key_projection_full = full_key.reshape(model_width, key_value_width)
    value_projection_full = full_value.reshape(model_width, key_value_width)
    w_output = full_output.reshape(q_width, model_width)
    inputs_f32 = inputs.reshape(row_count, model_width).astype(jnp.float32)
    unit_one, scale_one, first_normalized = norm_forward(inputs_f32, attn_gain)
    query_rows = apply_rotary(
        matrix_product(first_normalized, w_query).reshape(
            batch_count, sequence_length, QUERY_HEADS, HEAD_DIMENSION
        ),
        cosine_lookup,
        sine_lookup,
        1.0,
    )
    query_rows = query_rows.astype(jnp.bfloat16).reshape(
        batch_count, sequence_length, KEY_VALUE_HEADS, group_count, HEAD_DIMENSION
    )
    key_rows = apply_rotary(
        matrix_product(first_normalized, key_projection_full).reshape(
            batch_count, sequence_length, KEY_VALUE_HEADS, HEAD_DIMENSION
        ),
        cosine_lookup,
        sine_lookup,
        1.0,
    )
    key_rows = key_rows.astype(jnp.bfloat16)
    value_rows = (
        matrix_product(first_normalized, value_projection_full)
        .astype(jnp.bfloat16)
        .reshape(batch_count, sequence_length, KEY_VALUE_HEADS, HEAD_DIMENSION)
    )
    scores = masked_scores(query_rows, key_rows, causal, factor)
    row_top = jnp.max(scores, axis=-1, keepdims=True)
    log_total = row_top + jnp.log(jnp.sum(jnp.exp(scores - row_top), axis=-1, keepdims=True))
    probs = jnp.exp(scores - log_total).astype(jnp.bfloat16)
    attended = jnp.einsum(
        "bngqk,bknd->bqngd", probs, value_rows, preferred_element_type=jnp.float32
    )
    attended = attended.astype(jnp.bfloat16).reshape(row_count, q_width)
    hidden = inputs_f32 + matrix_product(attended, w_output)
    full_gate, full_up, full_down = (
        lax.all_gather(gate_weight, "fsdp", axis=0, tiled=True),
        lax.all_gather(up_weight, "fsdp", axis=0, tiled=True),
        lax.all_gather(down_weight, "fsdp", axis=0, tiled=True),
    )
    w_gate = full_gate.reshape(model_width, FEEDFORWARD_SIZE)
    w_up = full_up.reshape(model_width, FEEDFORWARD_SIZE)
    w_down = full_down.reshape(FEEDFORWARD_SIZE, model_width)
    unit_two, scale_two, normed_two = norm_forward(hidden, mlp_gain)
    gate = matrix_product(normed_two, w_gate)
    up_val = matrix_product(normed_two, w_up)
    sigmoid_gate = jax.nn.sigmoid(gate)
    activated = gate * sigmoid_gate
    mixed = (activated * up_val).astype(jnp.bfloat16)
    output = (
        (hidden + matrix_product(mixed, w_down))
        .astype(jnp.bfloat16)
        .reshape(batch_count, sequence_length, model_width)
    )
    again_gate, again_up, again_down = (
        lax.all_gather(gate_weight, "fsdp", axis=0, tiled=True),
        lax.all_gather(up_weight, "fsdp", axis=0, tiled=True),
        lax.all_gather(down_weight, "fsdp", axis=0, tiled=True),
    )
    w_gate = again_gate.reshape(model_width, FEEDFORWARD_SIZE)
    w_up = again_up.reshape(model_width, FEEDFORWARD_SIZE)
    w_down = again_down.reshape(FEEDFORWARD_SIZE, model_width)
    cotangent = out_cotangent.reshape(row_count, model_width)
    d_mixed = back_product(cotangent, w_down)
    d_gate = (d_mixed * up_val * (sigmoid_gate * (1.0 + gate * (1.0 - sigmoid_gate)))).astype(
        jnp.bfloat16
    )
    d_up = (d_mixed * activated).astype(jnp.bfloat16)
    mlp_pairs = [(normed_two, d_gate), (normed_two, d_up), (mixed, cotangent)]
    mlp_joined = lax.psum_scatter(
        gradient_term(mlp_pairs, devices, lax.axis_size("fsdp") * 1),
        "fsdp",
        scatter_dimension=0,
        tiled=True,
    )
    mlp_shards = split_shards(mlp_joined, mlp_pairs, devices)
    d_normed_two = back_product(d_gate, w_gate) + back_product(d_up, w_up)
    d_hid_norm, d_mlp_gain = norm_backward(d_normed_two, unit_two, scale_two, mlp_gain)
    d_hidden = cotangent.astype(jnp.float32) + d_hid_norm
    d_branch = d_hidden.astype(jnp.bfloat16)
    again_query, again_key, again_value, again_output = (
        lax.all_gather(query_weight, "fsdp", axis=0, tiled=True),
        lax.all_gather(key_matrix, "fsdp", axis=0, tiled=True),
        lax.all_gather(value_matrix, "fsdp", axis=0, tiled=True),
        lax.all_gather(output_weight, "fsdp", axis=0, tiled=True),
    )
    w_query = again_query.reshape(model_width, q_width)
    key_projection_full = again_key.reshape(model_width, key_value_width)
    value_projection_full = again_value.reshape(model_width, key_value_width)
    w_output = again_output.reshape(q_width, model_width)
    attended_gradient = back_product(d_branch, w_output).astype(jnp.bfloat16)
    attended_gradient = attended_gradient.reshape(
        batch_count, sequence_length, KEY_VALUE_HEADS, group_count, HEAD_DIMENSION
    )
    scores_again = masked_scores(query_rows, key_rows, causal, factor)
    probs_again = jnp.exp(scores_again - log_total).astype(jnp.bfloat16)
    d_probs = jnp.einsum(
        "bqngd,bknd->bngqk", attended_gradient, value_rows, preferred_element_type=jnp.float32
    )
    value_rows_gradient = jnp.einsum(
        "bngqk,bqngd->bknd", probs_again, attended_gradient, preferred_element_type=jnp.float32
    )
    probs_f32 = probs_again.astype(jnp.float32)
    delta = jnp.sum(probs_f32 * d_probs, axis=-1, keepdims=True)
    d_scores = (probs_f32 * (d_probs - delta) * factor).astype(jnp.bfloat16)
    d_queries = jnp.einsum(
        "bngqk,bknd->bqngd", d_scores, key_rows, preferred_element_type=jnp.float32
    )
    key_rows_gradient = jnp.einsum(
        "bngqk,bqngd->bknd", d_scores, query_rows, preferred_element_type=jnp.float32
    )
    d_queries = d_queries.reshape(batch_count, sequence_length, QUERY_HEADS, HEAD_DIMENSION)
    d_query_in = (
        apply_rotary(d_queries, cosine_lookup, sine_lookup, -1.0)
        .reshape(row_count, q_width)
        .astype(jnp.bfloat16)
    )
    key_input_gradient = (
        apply_rotary(key_rows_gradient, cosine_lookup, sine_lookup, -1.0)
        .reshape(row_count, key_value_width)
        .astype(jnp.bfloat16)
    )
    value_input_gradient = value_rows_gradient.reshape(row_count, key_value_width).astype(
        jnp.bfloat16
    )
    d_normed_one = (
        back_product(d_query_in, w_query)
        + back_product(key_input_gradient, key_projection_full)
        + back_product(value_input_gradient, value_projection_full)
    )
    d_in_norm, d_attn_gain = norm_backward(d_normed_one, unit_one, scale_one, attn_gain)
    input_grad = (d_hidden + d_in_norm).reshape(batch_count, sequence_length, model_width)
    attn_pairs = [
        (first_normalized, d_query_in),
        (first_normalized, key_input_gradient),
        (first_normalized, value_input_gradient),
        (attended, d_branch),
    ]
    attn_joined = lax.psum_scatter(
        gradient_term(attn_pairs, devices, lax.axis_size("fsdp") * 1),
        "fsdp",
        scatter_dimension=0,
        tiled=True,
    )
    shards = split_shards(attn_joined, attn_pairs, devices) + mlp_shards
    gain_sums = lax.psum((d_attn_gain, d_mlp_gain), "fsdp")
    return (
        output,
        input_grad,
        shards[0],
        shards[1],
        shards[2],
        shards[3],
        shards[4],
        shards[5],
        shards[6],
        gain_sums[0],
        gain_sums[1],
    )


PLANES = 4
TILE = 16


def unit_place(me):
    return me // 8, (me // 4) % 2, (me // 2) % 2, me % 2


def unit_index(z, y, x, c):
    return ((z * 2 + y) * 2 + x) * 2 + c


def partners(me):
    z, y, x, c = unit_place(me)
    peers = [unit_index((z + k) % PLANES, y, x, c) for k in range(1, PLANES)]
    peers.append(unit_index(z, y, 1 - x, c))
    peers.append(unit_index(z, 1 - y, x, c))
    peers.append(unit_index(z, y, x, 1 - c))
    return peers


def meet(peers):
    barrier = pltpu.get_barrier_semaphore()
    for peer in peers:
        pl.semaphore_signal(
            barrier, inc=1, device_id=(peer,), device_id_type=pl.DeviceIdType.MESH
        )
    pl.semaphore_wait(barrier, len(peers))


def remote(source, target, send, receive, device):
    return pltpu.make_async_remote_copy(
        src_ref=source,
        dst_ref=target,
        send_sem=send,
        recv_sem=receive,
        device_id=(device,),
        device_id_type=pl.DeviceIdType.MESH,
    )


def gather_kernel(count, *refs):
    shards, wholes = refs[:count], refs[count : 2 * count]
    send, receive, local = refs[2 * count :]
    me = lax.axis_index("fsdp")
    z, y, x, c = unit_place(me)
    meet(partners(me))
    over_x = unit_index(z, y, 1 - x, c)
    over_y = unit_index(z, 1 - y, x, c)

    def plane(k):
        return (z + PLANES - k) % PLANES

    def copy(a, slot, source, target, device):
        return remote(source, target, send.at[a, slot], receive.at[a, slot], device)

    def along_z(a, k):
        device = unit_index((z + k) % PLANES, y, x, c)
        return copy(a, k - 1, shards[a], wholes[a].at[z, y, x, c], device)

    def own(a, k, slot, device):
        target = wholes[a].at[plane(k), y, x, c]
        return copy(a, slot + k, shards[a] if k == 0 else target, target, device)

    def first(a, k):
        return own(a, k, 3, over_x if a % 2 == 0 else over_y)

    def second(a, k):
        return own(a, k, 7, over_y if a % 2 == 0 else over_x)

    def forward(a, k):
        if a % 2 == 0:
            part, device = wholes[a].at[plane(k), y, 1 - x, c], over_y
        else:
            part, device = wholes[a].at[plane(k), 1 - y, x, c], over_x
        return copy(a, 11 + k, part, part, device)

    def across(a):
        part = wholes[a].at[:, :, :, c]
        return copy(a, 15, part, part, unit_index(z, y, x, 1 - c))

    locals_ = [
        pltpu.make_async_copy(shards[a], wholes[a].at[z, y, x, c], local.at[a])
        for a in range(count)
    ]

    def begin(a):
        first(a, 0).start()
        second(a, 0).start()
        locals_[a].start()

    def pass_on(a):
        for k in range(1, PLANES):
            first(a, k).wait_recv()
            forward(a, k).start()

    def finish(a):
        for k in range(PLANES):
            second(a, k).wait_recv()
            forward(a, k).wait_recv()
        locals_[a].wait()
        across(a).start()

    for k in range(1, PLANES):
        along_z(0, k).start()
    begin(0)
    begin(1)
    for a in range(count):
        for k in range(1, PLANES):
            along_z(a, k).wait_recv()
        if a + 1 < count:
            for k in range(1, PLANES):
                along_z(a + 1, k).start()
        for k in range(1, PLANES):
            first(a, k).start()
            second(a, k).start()
        if a + 2 < count:
            begin(a + 2)
        first(a, 0).wait_recv()
        forward(a, 0).start()
        if a >= 1:
            pass_on(a - 1)
        if a >= 2:
            finish(a - 2)
    pass_on(count - 1)
    finish(count - 2)
    finish(count - 1)
    for a in range(count):
        across(a).wait_recv()
        across(a).wait_send()
        for k in range(PLANES):
            if k > 0:
                along_z(a, k).wait_send()
            first(a, k).wait_send()
            second(a, k).wait_send()
            forward(a, k).wait_send()


def gather_blocks(shards, identity):
    count = len(shards)
    return pl.pallas_call(
        functools.partial(gather_kernel, count),
        out_shape=[jax.ShapeDtypeStruct((PLANES, 2, 2, 2) + s.shape, s.dtype) for s in shards],
        in_specs=[pl.BlockSpec(memory_space=pl.ANY)] * count,
        out_specs=[pl.BlockSpec(memory_space=pl.ANY)] * count,
        scratch_shapes=[
            pltpu.SemaphoreType.DMA((count, 16)),
            pltpu.SemaphoreType.DMA((count, 16)),
            pltpu.SemaphoreType.DMA((count,)),
        ],
        compiler_params=pltpu.CompilerParams(collective_id=identity, has_side_effects=True),
    )(*shards)


def column_tiles(width, tile):
    return [(start, min(tile, width - start)) for start in range(0, width, tile)]


def scatter_kernel(plan, *refs):
    count = len(plan)
    factors = []
    used = 0
    for terms in plan:
        factors.append([(refs[used + 2 * i], refs[used + 2 * i + 1], at) for i, at in enumerate(terms)])
        used += 2 * len(terms)
    gain = refs[used]
    outs, gain_out = refs[used + 1 : used + 1 + count], refs[used + 1 + count]
    rest = refs[used + 2 + count :]
    grads, sibling, second, third, last = (rest[i * count : (i + 1) * count] for i in range(5))
    gain_a, gain_b, gain_c, gain_z, send, receive = rest[5 * count :]
    me = lax.axis_index("fsdp")
    z, y, x, c = unit_place(me)
    over_core = unit_index(z, y, x, 1 - c)
    over_x = unit_index(z, y, 1 - x, c)
    over_y = unit_index(z, 1 - y, x, c)
    meet(partners(me))

    def build(a):
        rows = grads[a].shape[4]

        @pl.loop(0, PLANES)
        def _(zz):
            for left, right, at in factors[a]:
                part = left[pl.ds(pl.multiple_of(zz * (8 * rows), 8 * rows), 8 * rows), :]
                for start, width in column_tiles(right.shape[1], 512):
                    value = jnp.dot(
                        part, right[:, start : start + width], preferred_element_type=jnp.float32
                    )
                    grads[a][zz, :, :, :, :, at + start : at + start + width] = value.astype(
                        grads[a].dtype
                    ).reshape(2, 2, 2, rows, width)

    def plane(k):
        return (z + k) % PLANES

    def copy(a, slot, source, target, device):
        return remote(source, target, send.at[a, slot], receive.at[a, slot], device)

    def across(a):
        return copy(a, 0, grads[a].at[:, :, :, 1 - c], sibling[a], over_core)

    def first(a, k):
        zz = plane(k)
        if a % 2 == 0:
            return copy(a, 1 + k, grads[a].at[zz, :, 1 - x, c], second[a].at[zz], over_x)
        return copy(a, 1 + k, grads[a].at[zz, 1 - y, :, c], second[a].at[zz], over_y)

    def after(a, k):
        zz = plane(k)
        if a % 2 == 0:
            return copy(a, 5 + k, grads[a].at[zz, 1 - y, x, c], third[a].at[zz], over_y)
        return copy(a, 5 + k, grads[a].at[zz, y, 1 - x, c], third[a].at[zz], over_x)

    def along_z(a, k):
        zz = plane(k)
        device = unit_index(zz, y, x, c)
        return copy(a, 8 + k, grads[a].at[zz, y, x, c], last[a].at[k - 1], device)

    def add(target, term):
        target[...] = (target[...].astype(jnp.float32) + term[...].astype(jnp.float32)).astype(
            target.dtype
        )

    def fold_core(a):
        across(a).wait_recv()

        @pl.loop(0, PLANES * 4)
        def _(i):
            zz, yy, xx = i // 4, (i // 2) % 2, i % 2
            add(grads[a].at[zz, yy, xx, c], sibling[a].at[zz, yy, xx])

    def fold_first(a, k):
        first(a, k).wait_recv()
        zz = plane(k)

        @pl.loop(0, 2)
        def _(other):
            if a % 2 == 0:
                add(grads[a].at[zz, other, x, c], second[a].at[zz, other])
            else:
                add(grads[a].at[zz, y, other, c], second[a].at[zz, other])

        after(a, k).start()

    def fold_after(a, k):
        after(a, k).wait_recv()
        zz = plane(k)
        add(grads[a].at[zz, y, x, c], third[a].at[zz])
        if k > 0:
            along_z(a, k).start()

    def gain_copies(phase):
        if phase < 3:
            source, target, device = (
                (gain, gain_a.at[1], over_core),
                (gain_a.at[0], gain_b.at[1], over_x),
                (gain_b.at[0], gain_c, over_y),
            )[phase]
            return [copy(count, phase, source, target, device)]
        return [
            copy(count, 2 + k, gain_z.at[z], gain_z.at[z], unit_index(plane(k), y, x, c))
            for k in range(1, PLANES)
        ]

    def gain_step(phase):
        for part in gain_copies(phase):
            part.wait_recv()
        if phase == 0:
            gain_a[0] = gain[...] + gain_a[1]
        elif phase == 1:
            gain_b[0] = gain_a[0] + gain_b[1]
        elif phase == 2:
            gain_z[z] = gain_b[0] + gain_c[...]
        else:
            gain_out[...] = (gain_z[0] + gain_z[1]) + (gain_z[2] + gain_z[3])
        if phase < 3:
            for part in gain_copies(phase + 1):
                part.start()

    gain_copies(0)[0].start()
    items = [
        (a, k) for pair in range(0, count, 2) for k in (1, 2, 3, 0) for a in (pair, pair + 1)
    ]
    window = 4
    folded = set()

    def release(item):
        if item[0] not in folded:
            fold_core(item[0])
            folded.add(item[0])
        first(*item).start()

    for a in range(2):
        build(a)
        across(a).start()
    for item in items[:window]:
        release(item)
    for a in range(2, count):
        build(a)
        across(a).start()
    for i, item in enumerate(items):
        fold_first(*item)
        if i + window < len(items):
            release(items[i + window])
        if i >= 2:
            fold_after(*items[i - 2])
        if i % 3 == 2 and i // 3 < 4:
            gain_step(i // 3)
    for item in items[-2:]:
        fold_after(*item)
    for a in range(count):
        total = grads[a][z, y, x, c].astype(jnp.float32)
        for k in range(1, PLANES):
            along_z(a, k).wait_recv()
            total = total + last[a][k - 1].astype(jnp.float32)
        outs[a][...] = total
    for a in range(count):
        across(a).wait_send()
        for k in range(PLANES):
            first(a, k).wait_send()
            after(a, k).wait_send()
            if k > 0:
                along_z(a, k).wait_send()
    for phase in range(4):
        for part in gain_copies(phase):
            part.wait_send()


def scatter_products(products, gain, devices, identity):
    plan, operands, blocks = [], [], []
    for terms in products:
        offsets, at = [], 0
        for left, right in terms:
            offsets.append(at)
            at += right.shape[1]
            operands += [left.T, right]
        plan.append(tuple(offsets))
        blocks.append((terms[0][0].shape[1] // devices, at))
    count = len(plan)
    vmem = pl.BlockSpec(memory_space=pltpu.VMEM)

    def room(lead):
        return [pltpu.VMEM(lead + b, jnp.bfloat16) for b in blocks]

    return pl.pallas_call(
        functools.partial(scatter_kernel, tuple(plan)),
        out_shape=[jax.ShapeDtypeStruct(b, jnp.float32) for b in blocks]
        + [jax.ShapeDtypeStruct(gain.shape, gain.dtype)],
        in_specs=[vmem] * (len(operands) + 1),
        out_specs=[vmem] * (count + 1),
        scratch_shapes=room((PLANES, 2, 2, 2))
        + room((PLANES, 2, 2))
        + room((PLANES, 2))
        + room((PLANES,))
        + room((PLANES - 1,))
        + [
            pltpu.VMEM((2,) + gain.shape, gain.dtype),
            pltpu.VMEM((2,) + gain.shape, gain.dtype),
            pltpu.VMEM(gain.shape, gain.dtype),
            pltpu.VMEM((PLANES,) + gain.shape, gain.dtype),
            pltpu.SemaphoreType.DMA((count + 1, 12)),
            pltpu.SemaphoreType.DMA((count + 1, 12)),
        ],
        compiler_params=pltpu.CompilerParams(
            collective_id=identity, has_side_effects=True, vmem_limit_bytes=56 * 1024 * 1024
        ),
    )(*operands, gain)


def spread_matrix(width, rows, padded_rows, devices):
    feature = jnp.arange(width)
    place = (feature // rows) * padded_rows + feature % rows
    return (place[:, None] == jnp.arange(devices * padded_rows)[None, :]).astype(jnp.bfloat16)


def widen(rows, spread):
    return matrix_product(rows.astype(jnp.bfloat16), spread).astype(jnp.bfloat16)


def narrow_exact(rows, spread):
    high = lax.reduce_precision(rows, 8, 7)
    middle = lax.reduce_precision(rows - high, 8, 7)
    low = rows - high - middle
    stacked = jnp.concatenate([high, middle, low], axis=0).astype(jnp.bfloat16)
    stacked = back_product(stacked, spread)
    count = rows.shape[0]
    return stacked[:count] + (stacked[count : 2 * count] + stacked[2 * count :])


def fast_body(
    inputs,
    out_cotangent,
    attn_gain,
    mlp_gain,
    query_weight,
    key_matrix,
    value_matrix,
    output_weight,
    gate_weight,
    up_weight,
    down_weight,
):
    _, sequence_length, model_width = inputs.shape
    tokens = sequence_length
    devices = lax.axis_size("fsdp")
    groups = QUERY_HEADS // KEY_VALUE_HEADS
    q_width = QUERY_HEADS * HEAD_DIMENSION
    kv_width = KEY_VALUE_HEADS * HEAD_DIMENSION
    factor = HEAD_DIMENSION ** (-0.5)
    rows = model_width // devices
    padded = -(-rows // TILE) * TILE
    down_rows = FEEDFORWARD_SIZE // devices
    cosine, sine = rope_tables(sequence_length, HEAD_DIMENSION // 2)
    causal = jnp.arange(sequence_length)[:, None] >= jnp.arange(sequence_length)[None, :]
    spread = spread_matrix(model_width, rows, padded, devices)

    def lay(weight):
        return weight.reshape(rows, -1)

    def fill(matrix):
        return jnp.pad(matrix, ((0, padded - rows), (0, 0)))

    qkv_width = q_width + 2 * kv_width
    gap = -qkv_width % 128
    attn_shard = fill(
        jnp.concatenate(
            [
                lay(query_weight),
                lay(key_matrix),
                jnp.pad(lay(value_matrix), ((0, 0), (0, gap))),
                lay(output_weight),
            ],
            axis=1,
        )
    )
    gathered = gather_blocks(
        [
            attn_shard,
            fill(lay(gate_weight)),
            fill(lay(up_weight)),
            down_weight.reshape(down_rows, model_width),
        ],
        0,
    )
    attn_all, w_gate, w_up, w_down = (g.reshape(-1, g.shape[-1]) for g in gathered)
    w_qkv = attn_all[:, :qkv_width]
    w_output = attn_all[:, qkv_width + gap :]

    x = inputs.reshape(tokens, model_width).astype(jnp.float32)
    cotangent = out_cotangent.reshape(tokens, model_width)
    unit_one, scale_one, normed_one = norm_forward(x, attn_gain)
    normed_one = widen(normed_one, spread)
    qkv = matrix_product(normed_one, w_qkv)
    queries = apply_rotary(
        qkv[:, :q_width].reshape(tokens, QUERY_HEADS, HEAD_DIMENSION), cosine, sine, 1.0
    )
    queries = queries.astype(jnp.bfloat16).reshape(1, tokens, KEY_VALUE_HEADS, groups, HEAD_DIMENSION)
    keys = apply_rotary(
        qkv[:, q_width : q_width + kv_width].reshape(tokens, KEY_VALUE_HEADS, HEAD_DIMENSION),
        cosine,
        sine,
        1.0,
    )
    keys = keys.astype(jnp.bfloat16)[None]
    values = (
        qkv[:, q_width + kv_width :]
        .astype(jnp.bfloat16)
        .reshape(1, tokens, KEY_VALUE_HEADS, HEAD_DIMENSION)
    )
    scores = masked_scores(queries, keys, causal, factor)
    row_top = jnp.max(scores, axis=-1, keepdims=True)
    log_total = row_top + jnp.log(jnp.sum(jnp.exp(scores - row_top), axis=-1, keepdims=True))
    probs = jnp.exp(scores - log_total).astype(jnp.bfloat16)
    attended = jnp.einsum("bngqk,bknd->bqngd", probs, values, preferred_element_type=jnp.float32)
    attended = widen(attended.astype(jnp.bfloat16).reshape(tokens, q_width), spread)
    hidden = x + matrix_product(attended, w_output)
    unit_two, scale_two, normed_two = norm_forward(hidden, mlp_gain)
    normed_two = widen(normed_two, spread)
    gate = matrix_product(normed_two, w_gate)
    up_val = matrix_product(normed_two, w_up)
    sigmoid_gate = jax.nn.sigmoid(gate)
    activated = gate * sigmoid_gate
    mixed = (activated * up_val).astype(jnp.bfloat16)
    output = (hidden + matrix_product(mixed, w_down)).astype(jnp.bfloat16)
    d_mixed = back_product(cotangent, w_down)
    d_gate = (d_mixed * up_val * (sigmoid_gate * (1.0 + gate * (1.0 - sigmoid_gate)))).astype(
        jnp.bfloat16
    )
    d_up = (d_mixed * activated).astype(jnp.bfloat16)

    d_normed_two = narrow_exact(back_product(d_gate, w_gate) + back_product(d_up, w_up), spread)
    d_hid_norm, d_mlp_gain = norm_backward(d_normed_two, unit_two, scale_two, mlp_gain)
    d_hidden = cotangent.astype(jnp.float32) + d_hid_norm
    d_branch = d_hidden.astype(jnp.bfloat16)
    d_attended = back_product(d_branch, w_output).astype(jnp.bfloat16)
    d_attended = back_product(d_attended, spread).astype(jnp.bfloat16)
    d_attended = d_attended.reshape(1, tokens, KEY_VALUE_HEADS, groups, HEAD_DIMENSION)
    d_probs = jnp.einsum("bqngd,bknd->bngqk", d_attended, values, preferred_element_type=jnp.float32)
    d_values = jnp.einsum("bngqk,bqngd->bknd", probs, d_attended, preferred_element_type=jnp.float32)
    probs_f32 = probs.astype(jnp.float32)
    delta = jnp.sum(probs_f32 * d_probs, axis=-1, keepdims=True)
    d_scores = (probs_f32 * (d_probs - delta) * factor).astype(jnp.bfloat16)
    d_queries = jnp.einsum("bngqk,bknd->bqngd", d_scores, keys, preferred_element_type=jnp.float32)
    d_keys = jnp.einsum("bngqk,bqngd->bknd", d_scores, queries, preferred_element_type=jnp.float32)
    d_query_in = apply_rotary(
        d_queries.reshape(tokens, QUERY_HEADS, HEAD_DIMENSION), cosine, sine, -1.0
    ).reshape(tokens, q_width)
    d_key_in = apply_rotary(
        d_keys.reshape(tokens, KEY_VALUE_HEADS, HEAD_DIMENSION), cosine, sine, -1.0
    ).reshape(tokens, kv_width)
    d_qkv = jnp.concatenate([d_query_in, d_key_in, d_values.reshape(tokens, kv_width)], axis=1)
    d_qkv = d_qkv.astype(jnp.bfloat16)
    d_normed_one = narrow_exact(back_product(d_qkv, w_qkv), spread)
    d_in_norm, d_attn_gain = norm_backward(d_normed_one, unit_one, scale_one, attn_gain)
    input_grad = d_hidden + d_in_norm
    gains = jnp.concatenate([d_attn_gain, d_mlp_gain])
    lanes = 128
    gain_rows = -(-gains.shape[0] // (8 * lanes)) * 8
    gains = jnp.pad(gains, (0, gain_rows * lanes - gains.shape[0])).reshape(gain_rows, lanes)

    products = [
        [(normed_two, d_gate)],
        [(normed_two, d_up)],
        [(mixed, cotangent)],
        [(normed_one, jnp.pad(d_qkv, ((0, 0), (0, gap)))), (attended, d_branch)],
    ]
    gate_part, up_part, down_part, attn_part, gain_sum = scatter_products(
        products, gains, devices, 1
    )
    attn_part = attn_part[:rows]
    gain_sum = gain_sum.reshape(-1)
    first, second = q_width, q_width + kv_width
    third = second + kv_width
    return (
        output.reshape(inputs.shape),
        input_grad.reshape(inputs.shape),
        attn_part[:, :first].reshape(-1),
        attn_part[:, first:second].reshape(-1),
        attn_part[:, second:third].reshape(-1),
        attn_part[:, third + gap :].reshape(-1),
        gate_part[:rows].reshape(-1),
        up_part[:rows].reshape(-1),
        down_part.reshape(-1),
        gain_sum[:model_width],
        gain_sum[model_width : 2 * model_width],
    )


def solution(mesh):
    in_specs = (
        P("fsdp", None, None),
        P("fsdp", None, None),
        P(),
        P(),
        P("fsdp"),
        P("fsdp"),
        P("fsdp"),
        P("fsdp"),
        P("fsdp"),
        P("fsdp"),
        P("fsdp"),
    )
    out_specs = (
        P("fsdp", None, None),
        P("fsdp", None, None),
        P("fsdp"),
        P("fsdp"),
        P("fsdp"),
        P("fsdp"),
        P("fsdp"),
        P("fsdp"),
        P("fsdp"),
        P(),
        P(),
    )
    chosen = fast_body if mesh.shape["fsdp"] == 8 * PLANES else body
    return jax.shard_map(
        chosen, mesh=mesh, in_specs=in_specs, out_specs=out_specs, check_vma=False)
```

```python
import functools

import jax
import jax.numpy as jnp
from jax import lax
from jax.experimental import pallas as pl
from jax.experimental.pallas import tpu as pltpu
from jax.sharding import PartitionSpec as P

QUERY_HEADS = 15
KEY_VALUE_HEADS = 5
HEAD_DIMENSION = 64
FEEDFORWARD_SIZE = 2560


EPS = 1e-05
THETA = 100000.0
MASKED = -1e30


def rope_tables(sequence_length, half_width):
    position = jnp.arange(sequence_length).astype(jnp.float32)
    freqs = THETA ** (-(jnp.arange(half_width).astype(jnp.float32) * 2.0) / (2.0 * half_width))
    angle = position[:, None] * freqs[None, :]
    return (jnp.cos(angle)[:, None, :], jnp.sin(angle)[:, None, :])


def apply_rotary(tensor, cosine_lookup, sine_lookup, rotation_sign):
    half_width = tensor.shape[-1] // 2
    first = tensor[..., :half_width]
    second = tensor[..., half_width:]
    return jnp.concatenate(
        [
            first * cosine_lookup - rotation_sign * second * sine_lookup,
            rotation_sign * first * sine_lookup + second * cosine_lookup,
        ],
        axis=-1,
    )


def norm_forward(value_rows, gain):
    scale = lax.rsqrt(jnp.mean(value_rows * value_rows, axis=-1, keepdims=True) + EPS)
    unit = value_rows * scale
    return (unit, scale, (unit * gain).astype(jnp.bfloat16))


def norm_backward(d_normed, unit, scale, gain):
    d_unit = d_normed * gain
    d_input = scale * (d_unit - unit * jnp.mean(d_unit * unit, axis=-1, keepdims=True))
    return (d_input, jnp.sum(d_normed * unit, axis=0))


def matrix_product(left, right):
    return jnp.dot(left, right, preferred_element_type=jnp.float32)


def back_product(left, right):
    return jnp.einsum("tf,df->td", left, right, preferred_element_type=jnp.float32)


def masked_scores(query_rows, key_rows, causal, factor):
    raw = (
        jnp.einsum("bqngd,bknd->bngqk", query_rows, key_rows, preferred_element_type=jnp.float32)
        * factor
    )
    return jnp.where(causal[None, None, None], raw, MASKED)


def flat_slice(left, right, count, stretch):
    product = jnp.einsum("tr,tf->rf", left, right, preferred_element_type=jnp.float32).reshape(-1)
    return product.reshape(count, stretch)


def gradient_term(pairs, devices, count):
    return jnp.concatenate(
        [
            flat_slice(left, right, count, left.shape[1] * right.shape[1] // devices)
            for left, right in pairs
        ],
        axis=1,
    )


def split_shards(joined, pairs, devices):
    pieces = []
    offset = 0
    for left, right in pairs:
        stretch = left.shape[1] * right.shape[1] // devices
        pieces.append(joined[0, offset : offset + stretch])
        offset = offset + stretch
    return pieces


def body(
    inputs,
    out_cotangent,
    attn_gain,
    mlp_gain,
    query_weight,
    key_matrix,
    value_matrix,
    output_weight,
    gate_weight,
    up_weight,
    down_weight,
):
    batch_count, sequence_length, model_width = inputs.shape
    row_count = batch_count * sequence_length
    devices = lax.axis_size("fsdp")
    group_count = QUERY_HEADS // KEY_VALUE_HEADS
    q_width = QUERY_HEADS * HEAD_DIMENSION
    key_value_width = KEY_VALUE_HEADS * HEAD_DIMENSION
    factor = HEAD_DIMENSION ** (-0.5)
    cosine_lookup, sine_lookup = rope_tables(sequence_length, HEAD_DIMENSION // 2)
    causal = jnp.arange(sequence_length)[:, None] >= jnp.arange(sequence_length)[None, :]
    full_query, full_key, full_value, full_output = (
        lax.all_gather(query_weight, "fsdp", axis=0, tiled=True),
        lax.all_gather(key_matrix, "fsdp", axis=0, tiled=True),
        lax.all_gather(value_matrix, "fsdp", axis=0, tiled=True),
        lax.all_gather(output_weight, "fsdp", axis=0, tiled=True),
    )
    w_query = full_query.reshape(model_width, q_width)
    key_projection_full = full_key.reshape(model_width, key_value_width)
    value_projection_full = full_value.reshape(model_width, key_value_width)
    w_output = full_output.reshape(q_width, model_width)
    inputs_f32 = inputs.reshape(row_count, model_width).astype(jnp.float32)
    unit_one, scale_one, first_normalized = norm_forward(inputs_f32, attn_gain)
    query_rows = apply_rotary(
        matrix_product(first_normalized, w_query).reshape(
            batch_count, sequence_length, QUERY_HEADS, HEAD_DIMENSION
        ),
        cosine_lookup,
        sine_lookup,
        1.0,
    )
    query_rows = query_rows.astype(jnp.bfloat16).reshape(
        batch_count, sequence_length, KEY_VALUE_HEADS, group_count, HEAD_DIMENSION
    )
    key_rows = apply_rotary(
        matrix_product(first_normalized, key_projection_full).reshape(
            batch_count, sequence_length, KEY_VALUE_HEADS, HEAD_DIMENSION
        ),
        cosine_lookup,
        sine_lookup,
        1.0,
    )
    key_rows = key_rows.astype(jnp.bfloat16)
    value_rows = (
        matrix_product(first_normalized, value_projection_full)
        .astype(jnp.bfloat16)
        .reshape(batch_count, sequence_length, KEY_VALUE_HEADS, HEAD_DIMENSION)
    )
    scores = masked_scores(query_rows, key_rows, causal, factor)
    row_top = jnp.max(scores, axis=-1, keepdims=True)
    log_total = row_top + jnp.log(jnp.sum(jnp.exp(scores - row_top), axis=-1, keepdims=True))
    probs = jnp.exp(scores - log_total).astype(jnp.bfloat16)
    attended = jnp.einsum(
        "bngqk,bknd->bqngd", probs, value_rows, preferred_element_type=jnp.float32
    )
    attended = attended.astype(jnp.bfloat16).reshape(row_count, q_width)
    hidden = inputs_f32 + matrix_product(attended, w_output)
    full_gate, full_up, full_down = (
        lax.all_gather(gate_weight, "fsdp", axis=0, tiled=True),
        lax.all_gather(up_weight, "fsdp", axis=0, tiled=True),
        lax.all_gather(down_weight, "fsdp", axis=0, tiled=True),
    )
    w_gate = full_gate.reshape(model_width, FEEDFORWARD_SIZE)
    w_up = full_up.reshape(model_width, FEEDFORWARD_SIZE)
    w_down = full_down.reshape(FEEDFORWARD_SIZE, model_width)
    unit_two, scale_two, normed_two = norm_forward(hidden, mlp_gain)
    gate = matrix_product(normed_two, w_gate)
    up_val = matrix_product(normed_two, w_up)
    sigmoid_gate = jax.nn.sigmoid(gate)
    activated = gate * sigmoid_gate
    mixed = (activated * up_val).astype(jnp.bfloat16)
    output = (
        (hidden + matrix_product(mixed, w_down))
        .astype(jnp.bfloat16)
        .reshape(batch_count, sequence_length, model_width)
    )
    again_gate, again_up, again_down = (
        lax.all_gather(gate_weight, "fsdp", axis=0, tiled=True),
        lax.all_gather(up_weight, "fsdp", axis=0, tiled=True),
        lax.all_gather(down_weight, "fsdp", axis=0, tiled=True),
    )
    w_gate = again_gate.reshape(model_width, FEEDFORWARD_SIZE)
    w_up = again_up.reshape(model_width, FEEDFORWARD_SIZE)
    w_down = again_down.reshape(FEEDFORWARD_SIZE, model_width)
    cotangent = out_cotangent.reshape(row_count, model_width)
    d_mixed = back_product(cotangent, w_down)
    d_gate = (d_mixed * up_val * (sigmoid_gate * (1.0 + gate * (1.0 - sigmoid_gate)))).astype(
        jnp.bfloat16
    )
    d_up = (d_mixed * activated).astype(jnp.bfloat16)
    mlp_pairs = [(normed_two, d_gate), (normed_two, d_up), (mixed, cotangent)]
    mlp_joined = lax.psum_scatter(
        gradient_term(mlp_pairs, devices, lax.axis_size("fsdp") * 1),
        "fsdp",
        scatter_dimension=0,
        tiled=True,
    )
    mlp_shards = split_shards(mlp_joined, mlp_pairs, devices)
    d_normed_two = back_product(d_gate, w_gate) + back_product(d_up, w_up)
    d_hid_norm, d_mlp_gain = norm_backward(d_normed_two, unit_two, scale_two, mlp_gain)
    d_hidden = cotangent.astype(jnp.float32) + d_hid_norm
    d_branch = d_hidden.astype(jnp.bfloat16)
    again_query, again_key, again_value, again_output = (
        lax.all_gather(query_weight, "fsdp", axis=0, tiled=True),
        lax.all_gather(key_matrix, "fsdp", axis=0, tiled=True),
        lax.all_gather(value_matrix, "fsdp", axis=0, tiled=True),
        lax.all_gather(output_weight, "fsdp", axis=0, tiled=True),
    )
    w_query = again_query.reshape(model_width, q_width)
    key_projection_full = again_key.reshape(model_width, key_value_width)
    value_projection_full = again_value.reshape(model_width, key_value_width)
    w_output = again_output.reshape(q_width, model_width)
    attended_gradient = back_product(d_branch, w_output).astype(jnp.bfloat16)
    attended_gradient = attended_gradient.reshape(
        batch_count, sequence_length, KEY_VALUE_HEADS, group_count, HEAD_DIMENSION
    )
    scores_again = masked_scores(query_rows, key_rows, causal, factor)
    probs_again = jnp.exp(scores_again - log_total).astype(jnp.bfloat16)
    d_probs = jnp.einsum(
        "bqngd,bknd->bngqk", attended_gradient, value_rows, preferred_element_type=jnp.float32
    )
    value_rows_gradient = jnp.einsum(
        "bngqk,bqngd->bknd", probs_again, attended_gradient, preferred_element_type=jnp.float32
    )
    probs_f32 = probs_again.astype(jnp.float32)
    delta = jnp.sum(probs_f32 * d_probs, axis=-1, keepdims=True)
    d_scores = (probs_f32 * (d_probs - delta) * factor).astype(jnp.bfloat16)
    d_queries = jnp.einsum(
        "bngqk,bknd->bqngd", d_scores, key_rows, preferred_element_type=jnp.float32
    )
    key_rows_gradient = jnp.einsum(
        "bngqk,bqngd->bknd", d_scores, query_rows, preferred_element_type=jnp.float32
    )
    d_queries = d_queries.reshape(batch_count, sequence_length, QUERY_HEADS, HEAD_DIMENSION)
    d_query_in = (
        apply_rotary(d_queries, cosine_lookup, sine_lookup, -1.0)
        .reshape(row_count, q_width)
        .astype(jnp.bfloat16)
    )
    key_input_gradient = (
        apply_rotary(key_rows_gradient, cosine_lookup, sine_lookup, -1.0)
        .reshape(row_count, key_value_width)
        .astype(jnp.bfloat16)
    )
    value_input_gradient = value_rows_gradient.reshape(row_count, key_value_width).astype(
        jnp.bfloat16
    )
    d_normed_one = (
        back_product(d_query_in, w_query)
        + back_product(key_input_gradient, key_projection_full)
        + back_product(value_input_gradient, value_projection_full)
    )
    d_in_norm, d_attn_gain = norm_backward(d_normed_one, unit_one, scale_one, attn_gain)
    input_grad = (d_hidden + d_in_norm).reshape(batch_count, sequence_length, model_width)
    attn_pairs = [
        (first_normalized, d_query_in),
        (first_normalized, key_input_gradient),
        (first_normalized, value_input_gradient),
        (attended, d_branch),
    ]
    attn_joined = lax.psum_scatter(
        gradient_term(attn_pairs, devices, lax.axis_size("fsdp") * 1),
        "fsdp",
        scatter_dimension=0,
        tiled=True,
    )
    shards = split_shards(attn_joined, attn_pairs, devices) + mlp_shards
    gain_sums = lax.psum((d_attn_gain, d_mlp_gain), "fsdp")
    return (
        output,
        input_grad,
        shards[0],
        shards[1],
        shards[2],
        shards[3],
        shards[4],
        shards[5],
        shards[6],
        gain_sums[0],
        gain_sums[1],
    )


PLANES = 4
TILE = 16


def unit_place(me):
    return me // 8, (me // 4) % 2, (me // 2) % 2, me % 2


def unit_index(z, y, x, c):
    return ((z * 2 + y) * 2 + x) * 2 + c


def partners(me):
    z, y, x, c = unit_place(me)
    peers = [unit_index((z + k) % PLANES, y, x, c) for k in range(1, PLANES)]
    peers.append(unit_index(z, y, 1 - x, c))
    peers.append(unit_index(z, 1 - y, x, c))
    peers.append(unit_index(z, y, x, 1 - c))
    return peers


def meet(peers):
    barrier = pltpu.get_barrier_semaphore()
    for peer in peers:
        pl.semaphore_signal(
            barrier, inc=1, device_id=(peer,), device_id_type=pl.DeviceIdType.MESH
        )
    pl.semaphore_wait(barrier, len(peers))


def remote(source, target, send, receive, device):
    return pltpu.make_async_remote_copy(
        src_ref=source,
        dst_ref=target,
        send_sem=send,
        recv_sem=receive,
        device_id=(device,),
        device_id_type=pl.DeviceIdType.MESH,
    )


def gather_kernel(count, *refs):
    shards, wholes = refs[:count], refs[count : 2 * count]
    send, receive, local = refs[2 * count :]
    me = lax.axis_index("fsdp")
    z, y, x, c = unit_place(me)
    meet(partners(me))
    over_x = unit_index(z, y, 1 - x, c)
    over_y = unit_index(z, 1 - y, x, c)

    def plane(k):
        return (z + PLANES - k) % PLANES

    def copy(a, slot, source, target, device):
        return remote(source, target, send.at[a, slot], receive.at[a, slot], device)

    def along_z(a, k):
        device = unit_index((z + k) % PLANES, y, x, c)
        return copy(a, k - 1, shards[a], wholes[a].at[z, y, x, c], device)

    def own(a, k, slot, device):
        target = wholes[a].at[plane(k), y, x, c]
        return copy(a, slot + k, shards[a] if k == 0 else target, target, device)

    def first(a, k):
        return own(a, k, 3, over_x if a % 2 == 0 else over_y)

    def second(a, k):
        return own(a, k, 7, over_y if a % 2 == 0 else over_x)

    def forward(a, k):
        if a % 2 == 0:
            part, device = wholes[a].at[plane(k), y, 1 - x, c], over_y
        else:
            part, device = wholes[a].at[plane(k), 1 - y, x, c], over_x
        return copy(a, 11 + k, part, part, device)

    def across(a):
        part = wholes[a].at[:, :, :, c]
        return copy(a, 15, part, part, unit_index(z, y, x, 1 - c))

    locals_ = [
        pltpu.make_async_copy(shards[a], wholes[a].at[z, y, x, c], local.at[a])
        for a in range(count)
    ]

    def begin(a):
        first(a, 0).start()
        second(a, 0).start()
        locals_[a].start()

    def pass_on(a):
        for k in range(1, PLANES):
            first(a, k).wait_recv()
            forward(a, k).start()

    def finish(a):
        for k in range(PLANES):
            second(a, k).wait_recv()
            forward(a, k).wait_recv()
        locals_[a].wait()
        across(a).start()

    for k in range(1, PLANES):
        along_z(0, k).start()
    begin(0)
    begin(1)
    for a in range(count):
        for k in range(1, PLANES):
            along_z(a, k).wait_recv()
        if a + 1 < count:
            for k in range(1, PLANES):
                along_z(a + 1, k).start()
        for k in range(1, PLANES):
            first(a, k).start()
            second(a, k).start()
        if a + 2 < count:
            begin(a + 2)
        first(a, 0).wait_recv()
        forward(a, 0).start()
        if a >= 1:
            pass_on(a - 1)
        if a >= 2:
            finish(a - 2)
    pass_on(count - 1)
    finish(count - 2)
    finish(count - 1)
    for a in range(count):
        across(a).wait_recv()
        across(a).wait_send()
        for k in range(PLANES):
            if k > 0:
                along_z(a, k).wait_send()
            first(a, k).wait_send()
            second(a, k).wait_send()
            forward(a, k).wait_send()


def gather_blocks(shards, identity):
    count = len(shards)
    return pl.pallas_call(
        functools.partial(gather_kernel, count),
        out_shape=[jax.ShapeDtypeStruct((PLANES, 2, 2, 2) + s.shape, s.dtype) for s in shards],
        in_specs=[pl.BlockSpec(memory_space=pl.ANY)] * count,
        out_specs=[pl.BlockSpec(memory_space=pl.ANY)] * count,
        scratch_shapes=[
            pltpu.SemaphoreType.DMA((count, 16)),
            pltpu.SemaphoreType.DMA((count, 16)),
            pltpu.SemaphoreType.DMA((count,)),
        ],
        compiler_params=pltpu.CompilerParams(collective_id=identity, has_side_effects=True),
    )(*shards)


def column_tiles(width, tile):
    return [(start, min(tile, width - start)) for start in range(0, width, tile)]


def scatter_kernel(plan, *refs):
    count = len(plan)
    factors = []
    used = 0
    for terms in plan:
        factors.append([(refs[used + 2 * i], refs[used + 2 * i + 1], at) for i, at in enumerate(terms)])
        used += 2 * len(terms)
    gain = refs[used]
    outs, gain_out = refs[used + 1 : used + 1 + count], refs[used + 1 + count]
    rest = refs[used + 2 + count :]
    grads, sibling, second, third, last = (rest[i * count : (i + 1) * count] for i in range(5))
    gain_a, gain_b, gain_c, gain_z, send, receive = rest[5 * count :]
    me = lax.axis_index("fsdp")
    z, y, x, c = unit_place(me)
    over_core = unit_index(z, y, x, 1 - c)
    over_x = unit_index(z, y, 1 - x, c)
    over_y = unit_index(z, 1 - y, x, c)
    meet(partners(me))

    def plane(k):
        return (z + k) % PLANES

    def build(a, k):
        rows = grads[a].shape[4]
        zz = plane(k)
        for left, right, at in factors[a]:
            part = left[pl.ds(pl.multiple_of(zz * (8 * rows), 8 * rows), 8 * rows), :]
            for start, width in column_tiles(right.shape[1], 512):
                value = jnp.dot(
                    part, right[:, start : start + width], preferred_element_type=jnp.float32
                )
                grads[a][zz, :, :, :, :, at + start : at + start + width] = value.astype(
                    grads[a].dtype
                ).reshape(2, 2, 2, rows, width)
        across(a, k).start()

    def copy(a, slot, source, target, device):
        return remote(source, target, send.at[a, slot], receive.at[a, slot], device)

    def across(a, k):
        zz = plane(k)
        return copy(a, 12 + k, grads[a].at[zz, :, :, 1 - c], sibling[a].at[zz], over_core)

    def first(a, k):
        zz = plane(k)
        if a % 2 == 0:
            return copy(a, 1 + k, grads[a].at[zz, :, 1 - x, c], second[a].at[zz], over_x)
        return copy(a, 1 + k, grads[a].at[zz, 1 - y, :, c], second[a].at[zz], over_y)

    def after(a, k):
        zz = plane(k)
        if a % 2 == 0:
            return copy(a, 5 + k, grads[a].at[zz, 1 - y, x, c], third[a].at[zz], over_y)
        return copy(a, 5 + k, grads[a].at[zz, y, 1 - x, c], third[a].at[zz], over_x)

    def along_z(a, k):
        zz = plane(k)
        device = unit_index(zz, y, x, c)
        return copy(a, 8 + k, grads[a].at[zz, y, x, c], last[a].at[k - 1], device)

    def add(target, term):
        target[...] = (target[...].astype(jnp.float32) + term[...].astype(jnp.float32)).astype(
            target.dtype
        )

    def fold_core(a, k):
        across(a, k).wait_recv()
        zz = plane(k)

        @pl.loop(0, 4)
        def _(i):
            yy, xx = i // 2, i % 2
            add(grads[a].at[zz, yy, xx, c], sibling[a].at[zz, yy, xx])

    def fold_first(a, k):
        first(a, k).wait_recv()
        zz = plane(k)

        @pl.loop(0, 2)
        def _(other):
            if a % 2 == 0:
                add(grads[a].at[zz, other, x, c], second[a].at[zz, other])
            else:
                add(grads[a].at[zz, y, other, c], second[a].at[zz, other])

        after(a, k).start()

    def fold_after(a, k):
        after(a, k).wait_recv()
        zz = plane(k)
        add(grads[a].at[zz, y, x, c], third[a].at[zz])
        if k > 0:
            along_z(a, k).start()

    def gain_copies(phase):
        if phase < 3:
            source, target, device = (
                (gain, gain_a.at[1], over_core),
                (gain_a.at[0], gain_b.at[1], over_x),
                (gain_b.at[0], gain_c, over_y),
            )[phase]
            return [copy(count, phase, source, target, device)]
        return [
            copy(count, 2 + k, gain_z.at[z], gain_z.at[z], unit_index(plane(k), y, x, c))
            for k in range(1, PLANES)
        ]

    def gain_step(phase):
        for part in gain_copies(phase):
            part.wait_recv()
        if phase == 0:
            gain_a[0] = gain[...] + gain_a[1]
        elif phase == 1:
            gain_b[0] = gain_a[0] + gain_b[1]
        elif phase == 2:
            gain_z[z] = gain_b[0] + gain_c[...]
        else:
            gain_out[...] = (gain_z[0] + gain_z[1]) + (gain_z[2] + gain_z[3])
        if phase < 3:
            for part in gain_copies(phase + 1):
                part.start()

    gain_copies(0)[0].start()
    items = [
        (a, k) for pair in range(0, count, 2) for k in (1, 2, 3, 0) for a in (pair, pair + 1)
    ]
    window, ahead = 5, 3

    def release(i):
        fold_core(*items[i])
        first(*items[i]).start()
        if i + ahead < len(items):
            build(*items[i + ahead])

    for item in items[:ahead]:
        build(*item)
    for i in range(window):
        release(i)
    for i, item in enumerate(items):
        fold_first(*item)
        if i + window < len(items):
            release(i + window)
        if i >= 2:
            fold_after(*items[i - 2])
        if i % 3 == 2 and i // 3 < 4:
            gain_step(i // 3)
    for item in items[-2:]:
        fold_after(*item)
    for a in range(count):
        total = grads[a][z, y, x, c].astype(jnp.float32)
        for k in range(1, PLANES):
            along_z(a, k).wait_recv()
            total = total + last[a][k - 1].astype(jnp.float32)
        outs[a][...] = total
    for a in range(count):
        for k in range(PLANES):
            across(a, k).wait_send()
            first(a, k).wait_send()
            after(a, k).wait_send()
            if k > 0:
                along_z(a, k).wait_send()
    for phase in range(4):
        for part in gain_copies(phase):
            part.wait_send()


def scatter_products(products, gain, devices, identity):
    plan, operands, blocks = [], [], []
    for terms in products:
        offsets, at = [], 0
        for left, right in terms:
            offsets.append(at)
            at += right.shape[1]
            operands += [left.T, right]
        plan.append(tuple(offsets))
        blocks.append((terms[0][0].shape[1] // devices, at))
    count = len(plan)
    vmem = pl.BlockSpec(memory_space=pltpu.VMEM)

    def room(lead):
        return [pltpu.VMEM(lead + b, jnp.bfloat16) for b in blocks]

    return pl.pallas_call(
        functools.partial(scatter_kernel, tuple(plan)),
        out_shape=[jax.ShapeDtypeStruct(b, jnp.float32) for b in blocks]
        + [jax.ShapeDtypeStruct(gain.shape, gain.dtype)],
        in_specs=[vmem] * (len(operands) + 1),
        out_specs=[vmem] * (count + 1),
        scratch_shapes=room((PLANES, 2, 2, 2))
        + room((PLANES, 2, 2))
        + room((PLANES, 2))
        + room((PLANES,))
        + room((PLANES - 1,))
        + [
            pltpu.VMEM((2,) + gain.shape, gain.dtype),
            pltpu.VMEM((2,) + gain.shape, gain.dtype),
            pltpu.VMEM(gain.shape, gain.dtype),
            pltpu.VMEM((PLANES,) + gain.shape, gain.dtype),
            pltpu.SemaphoreType.DMA((count + 1, 16)),
            pltpu.SemaphoreType.DMA((count + 1, 16)),
        ],
        compiler_params=pltpu.CompilerParams(
            collective_id=identity, has_side_effects=True, vmem_limit_bytes=56 * 1024 * 1024
        ),
    )(*operands, gain)


def spread_matrix(width, rows, padded_rows, devices):
    feature = jnp.arange(width)
    place = (feature // rows) * padded_rows + feature % rows
    return (place[:, None] == jnp.arange(devices * padded_rows)[None, :]).astype(jnp.bfloat16)


def widen(rows, spread):
    return matrix_product(rows.astype(jnp.bfloat16), spread).astype(jnp.bfloat16)


def narrow_exact(rows, spread):
    high = lax.reduce_precision(rows, 8, 7)
    middle = lax.reduce_precision(rows - high, 8, 7)
    low = rows - high - middle
    stacked = jnp.concatenate([high, middle, low], axis=0).astype(jnp.bfloat16)
    stacked = back_product(stacked, spread)
    count = rows.shape[0]
    return stacked[:count] + (stacked[count : 2 * count] + stacked[2 * count :])


def fast_body(
    inputs,
    out_cotangent,
    attn_gain,
    mlp_gain,
    query_weight,
    key_matrix,
    value_matrix,
    output_weight,
    gate_weight,
    up_weight,
    down_weight,
):
    _, sequence_length, model_width = inputs.shape
    tokens = sequence_length
    devices = lax.axis_size("fsdp")
    groups = QUERY_HEADS // KEY_VALUE_HEADS
    q_width = QUERY_HEADS * HEAD_DIMENSION
    kv_width = KEY_VALUE_HEADS * HEAD_DIMENSION
    factor = HEAD_DIMENSION ** (-0.5)
    rows = model_width // devices
    padded = -(-rows // TILE) * TILE
    down_rows = FEEDFORWARD_SIZE // devices
    cosine, sine = rope_tables(sequence_length, HEAD_DIMENSION // 2)
    causal = jnp.arange(sequence_length)[:, None] >= jnp.arange(sequence_length)[None, :]
    spread = spread_matrix(model_width, rows, padded, devices)

    def lay(weight):
        return weight.reshape(rows, -1)

    def fill(matrix):
        return jnp.pad(matrix, ((0, padded - rows), (0, 0)))

    qkv_width = q_width + 2 * kv_width
    gap = -qkv_width % 128
    attn_shard = fill(
        jnp.concatenate(
            [
                lay(query_weight),
                lay(key_matrix),
                jnp.pad(lay(value_matrix), ((0, 0), (0, gap))),
                lay(output_weight),
            ],
            axis=1,
        )
    )
    gathered = gather_blocks(
        [
            attn_shard,
            fill(lay(gate_weight)),
            fill(lay(up_weight)),
            down_weight.reshape(down_rows, model_width),
        ],
        0,
    )
    attn_all, w_gate, w_up, w_down = (g.reshape(-1, g.shape[-1]) for g in gathered)
    w_qkv = attn_all[:, :qkv_width]
    w_output = attn_all[:, qkv_width + gap :]

    x = inputs.reshape(tokens, model_width).astype(jnp.float32)
    cotangent = out_cotangent.reshape(tokens, model_width)
    unit_one, scale_one, normed_one = norm_forward(x, attn_gain)
    normed_one = widen(normed_one, spread)
    qkv = matrix_product(normed_one, w_qkv)
    queries = apply_rotary(
        qkv[:, :q_width].reshape(tokens, QUERY_HEADS, HEAD_DIMENSION), cosine, sine, 1.0
    )
    queries = queries.astype(jnp.bfloat16).reshape(1, tokens, KEY_VALUE_HEADS, groups, HEAD_DIMENSION)
    keys = apply_rotary(
        qkv[:, q_width : q_width + kv_width].reshape(tokens, KEY_VALUE_HEADS, HEAD_DIMENSION),
        cosine,
        sine,
        1.0,
    )
    keys = keys.astype(jnp.bfloat16)[None]
    values = (
        qkv[:, q_width + kv_width :]
        .astype(jnp.bfloat16)
        .reshape(1, tokens, KEY_VALUE_HEADS, HEAD_DIMENSION)
    )
    scores = masked_scores(queries, keys, causal, factor)
    row_top = jnp.max(scores, axis=-1, keepdims=True)
    log_total = row_top + jnp.log(jnp.sum(jnp.exp(scores - row_top), axis=-1, keepdims=True))
    probs = jnp.exp(scores - log_total).astype(jnp.bfloat16)
    attended = jnp.einsum("bngqk,bknd->bqngd", probs, values, preferred_element_type=jnp.float32)
    attended = widen(attended.astype(jnp.bfloat16).reshape(tokens, q_width), spread)
    hidden = x + matrix_product(attended, w_output)
    unit_two, scale_two, normed_two = norm_forward(hidden, mlp_gain)
    normed_two = widen(normed_two, spread)
    gate = matrix_product(normed_two, w_gate)
    up_val = matrix_product(normed_two, w_up)
    sigmoid_gate = jax.nn.sigmoid(gate)
    activated = gate * sigmoid_gate
    mixed = (activated * up_val).astype(jnp.bfloat16)
    output = (hidden + matrix_product(mixed, w_down)).astype(jnp.bfloat16)
    d_mixed = back_product(cotangent, w_down)
    d_gate = (d_mixed * up_val * (sigmoid_gate * (1.0 + gate * (1.0 - sigmoid_gate)))).astype(
        jnp.bfloat16
    )
    d_up = (d_mixed * activated).astype(jnp.bfloat16)

    d_normed_two = narrow_exact(back_product(d_gate, w_gate) + back_product(d_up, w_up), spread)
    d_hid_norm, d_mlp_gain = norm_backward(d_normed_two, unit_two, scale_two, mlp_gain)
    d_hidden = cotangent.astype(jnp.float32) + d_hid_norm
    d_branch = d_hidden.astype(jnp.bfloat16)
    d_attended = back_product(d_branch, w_output).astype(jnp.bfloat16)
    d_attended = back_product(d_attended, spread).astype(jnp.bfloat16)
    d_attended = d_attended.reshape(1, tokens, KEY_VALUE_HEADS, groups, HEAD_DIMENSION)
    d_probs = jnp.einsum("bqngd,bknd->bngqk", d_attended, values, preferred_element_type=jnp.float32)
    d_values = jnp.einsum("bngqk,bqngd->bknd", probs, d_attended, preferred_element_type=jnp.float32)
    probs_f32 = probs.astype(jnp.float32)
    delta = jnp.sum(probs_f32 * d_probs, axis=-1, keepdims=True)
    d_scores = (probs_f32 * (d_probs - delta) * factor).astype(jnp.bfloat16)
    d_queries = jnp.einsum("bngqk,bknd->bqngd", d_scores, keys, preferred_element_type=jnp.float32)
    d_keys = jnp.einsum("bngqk,bqngd->bknd", d_scores, queries, preferred_element_type=jnp.float32)
    d_query_in = apply_rotary(
        d_queries.reshape(tokens, QUERY_HEADS, HEAD_DIMENSION), cosine, sine, -1.0
    ).reshape(tokens, q_width)
    d_key_in = apply_rotary(
        d_keys.reshape(tokens, KEY_VALUE_HEADS, HEAD_DIMENSION), cosine, sine, -1.0
    ).reshape(tokens, kv_width)
    d_qkv = jnp.concatenate([d_query_in, d_key_in, d_values.reshape(tokens, kv_width)], axis=1)
    d_qkv = d_qkv.astype(jnp.bfloat16)
    d_normed_one = narrow_exact(back_product(d_qkv, w_qkv), spread)
    d_in_norm, d_attn_gain = norm_backward(d_normed_one, unit_one, scale_one, attn_gain)
    input_grad = d_hidden + d_in_norm
    gains = jnp.concatenate([d_attn_gain, d_mlp_gain])
    lanes = 128
    gain_rows = -(-gains.shape[0] // (8 * lanes)) * 8
    gains = jnp.pad(gains, (0, gain_rows * lanes - gains.shape[0])).reshape(gain_rows, lanes)

    products = [
        [(normed_two, d_gate)],
        [(normed_two, d_up)],
        [(mixed, cotangent)],
        [(normed_one, jnp.pad(d_qkv, ((0, 0), (0, gap)))), (attended, d_branch)],
    ]
    gate_part, up_part, down_part, attn_part, gain_sum = scatter_products(
        products, gains, devices, 1
    )
    attn_part = attn_part[:rows]
    gain_sum = gain_sum.reshape(-1)
    first, second = q_width, q_width + kv_width
    third = second + kv_width
    return (
        output.reshape(inputs.shape),
        input_grad.reshape(inputs.shape),
        attn_part[:, :first].reshape(-1),
        attn_part[:, first:second].reshape(-1),
        attn_part[:, second:third].reshape(-1),
        attn_part[:, third + gap :].reshape(-1),
        gate_part[:rows].reshape(-1),
        up_part[:rows].reshape(-1),
        down_part.reshape(-1),
        gain_sum[:model_width],
        gain_sum[model_width : 2 * model_width],
    )


def solution(mesh):
    in_specs = (
        P("fsdp", None, None),
        P("fsdp", None, None),
        P(),
        P(),
        P("fsdp"),
        P("fsdp"),
        P("fsdp"),
        P("fsdp"),
        P("fsdp"),
        P("fsdp"),
        P("fsdp"),
    )
    out_specs = (
        P("fsdp", None, None),
        P("fsdp", None, None),
        P("fsdp"),
        P("fsdp"),
        P("fsdp"),
        P("fsdp"),
        P("fsdp"),
        P("fsdp"),
        P("fsdp"),
        P(),
        P(),
    )
    chosen = fast_body if mesh.shape["fsdp"] == 8 * PLANES else body
    return jax.shard_map(
        chosen, mesh=mesh, in_specs=in_specs, out_specs=out_specs, check_vma=False)
```
